32 devices in a mesh: section: 4 (over x, core), head: 4 (over z), kv: 2 (over y).
Axes of the slice: x: 2, y: 2, z: 4, core: 2. Of those that a mesh axis runs over, the one named last changes fastest.
Arguments:
- tokens: bfloat16 [4, 256, 4096], P('section', 'kv', 'head'), may hold values from -40 to 40
- w_query: bfloat16 [4096, 4096], P(('section', 'kv'), 'head'), may hold values from -0.21875 to 0.21875
- w_keyvalue: bfloat16 [4096, 2, 4096], P(('section', 'kv'), None, 'head'), may hold values from -0.09375 to 0.09375
- cache_keys: bfloat16 [4, 4096, 4096], P('section', 'kv', 'head'), may hold values from -800 to 800
- cache_values: bfloat16 [4, 4096, 4096], P('section', 'kv', 'head'), may hold values from -6 to 6
- key_start: int32 [4], P('section'), may hold values from 0 to 2047
- key_end: int32 [4], P('section'), may hold values from 3072 to 4096
- w_out: bfloat16 [4096, 4096], P('head', ('section', 'kv')), may hold values from -0.375 to 0.375
Outputs:
- attention_out: bfloat16 [4, 256, 4096], P('section', 'kv', 'head')
The draws below stay inside these ranges and needn't reach their ends.
All inputs are finite; a program needn't handle non-finite values.
Results may differ from the reference program's by a relative error of at most 0.014.
The reference program's roundings to bfloat16 on the way (of `normed`, `queries`, `weights` and `attended`) count: a program that leaves them out, or rounds other values in their place, can miss the bound.
Values may be sent and summed in bfloat16 or wider, within the bound.
A program may use at most 128 MiB of HBM per device.

```python
import jax
import jax.numpy as jnp
from jax import lax

D = 4096
H = 32
HD = 128
SAMPLES = 4
NEW = 256
CTX = 4096


def draw_tokens(key, part):
    base_key, column_key, row_key = jax.random.split(jax.random.fold_in(key, 11), 3)
    column_scale = jnp.exp(jax.random.uniform(column_key, (1, 1, D), jnp.float32, -1.15, 1.15))
    row_scale = jnp.exp(jax.random.uniform(row_key, (SAMPLES, NEW, 1), jnp.float32, -0.8, 0.8))
    base_draw = jax.random.normal(base_key, (SAMPLES, NEW, D), jnp.float32)
    return jnp.clip(base_draw * column_scale * row_scale, -40.0, 40.0).astype(jnp.bfloat16)


def draw_cache_keys(key, part):
    base_key = jax.random.fold_in(jax.random.fold_in(key, 23), 0)
    base_draw = jax.random.normal(base_key, (SAMPLES, CTX, D), jnp.float32)
    return jnp.clip(base_draw, -6.0, 6.0).astype(jnp.bfloat16)


def with_ends(entries, rng, least, high):
    place = [jax.random.randint(jax.random.fold_in(rng, axis), (), 0, length) for axis, length in enumerate(entries.shape)]
    widest = entries.shape.index(max(entries.shape))
    beside = place[:widest] + [(place[widest] + 1) % entries.shape[widest]] + place[widest + 1:]
    return entries.at[tuple(place)].set(least).at[tuple(beside)].set(high)


def level_of(stream_key, shape, cuts, smallest, high):
    level, own = 1.0, jax.random.fold_in(stream_key, 6)
    for dim, blocks in cuts:
        steps = jnp.exp(jax.random.uniform(jax.random.fold_in(own, dim), (blocks,), jnp.float32, smallest / len(cuts), high / len(cuts)))
        level = level * jnp.repeat(steps, shape[dim] // blocks).reshape([-1 if axis == dim else 1 for axis in range(len(shape))])
    return level


def bell_draw(stream_key, extent, width, most, cuts=(), kind=jnp.bfloat16):
    level = level_of(stream_key, extent, cuts, -0.22, 0.18) if cuts else 1.0
    entries = jax.random.normal(stream_key, extent, jnp.float32) * width * level
    return jnp.minimum(jnp.maximum(entries, -most), most).astype(kind)


def setup_inputs(seed: int = 0) -> dict:
    splits = jax.random.split(jax.random.key(seed), 9)
    return {
        "tokens": draw_tokens(jax.random.fold_in(splits[8], 71), 0),
        "w_query": bell_draw(splits[1], (D, D), (D // 5) ** -0.5, 0.21875, ((0, 8), (1, 4))),
        "w_keyvalue": bell_draw(splits[2], (D, 2, D), D ** -0.5, 0.09375, ((0, 8), (2, 4))),
        "cache_keys": draw_cache_keys(jax.random.fold_in(splits[8], 71), 0),
        "cache_values": bell_draw(splits[4], (SAMPLES, CTX, D), 1.0, 6.0, ((0, 4), (1, 2), (2, 4))),
        "key_start": with_ends(jax.random.randint(splits[5], (SAMPLES,), 0, CTX // 2), jax.random.fold_in(splits[5], 1), 0, (CTX // 2) - 1).astype(jnp.int32),
        "key_end": with_ends(jax.random.randint(splits[6], (SAMPLES,), 3 * CTX // 4, CTX + 1), jax.random.fold_in(splits[6], 1), 3 * CTX // 4, CTX).astype(jnp.int32),
        "w_out": bell_draw(splits[7], (D, D), (D // 16) ** -0.5, 0.375, ((0, 4), (1, 8))),
    }


def reference(tokens, w_query, w_keyvalue, cache_keys, cache_values, key_start, key_end, w_out):
    widened = tokens.astype(jnp.float32)
    scaled = widened * lax.rsqrt(lax.optimization_barrier(jnp.mean(widened * widened, axis=2, keepdims=True)) + 1e-05)
    normed = scaled.astype(jnp.bfloat16).reshape(SAMPLES * NEW, D)
    queries = jnp.dot(normed, w_query, preferred_element_type=jnp.float32).astype(jnp.bfloat16)
    pair_sums = jnp.dot(normed, w_keyvalue.reshape(D, 2 * D), preferred_element_type=jnp.float32).astype(jnp.bfloat16)
    queries = queries.reshape(SAMPLES, NEW, H, HD)
    new_keys = pair_sums[:, :D].reshape(SAMPLES, NEW, H, HD)
    new_values = pair_sums[:, D:].reshape(SAMPLES, NEW, H, HD)
    keys_all = jnp.concatenate([cache_keys.reshape(SAMPLES, CTX, H, HD), new_keys], axis=1)
    values_all = jnp.concatenate([cache_values.reshape(SAMPLES, CTX, H, HD), new_values], axis=1)
    key_place = jnp.arange(CTX + NEW, dtype=jnp.int32)
    row_place = jnp.arange(NEW, dtype=jnp.int32)
    score_scale = HD ** (-0.5)

    def one_sample(packed):
        query_sample, keys_sample, values_sample, window_begin, window_stop = packed
        cache_usable = (key_place < CTX) & (key_place >= window_begin) & (key_place < window_stop)
        new_usable = (key_place[None, :] >= CTX) & (key_place[None, :] - CTX <= row_place[:, None])
        usable = cache_usable[None, :] | new_usable

        def one_head(head_pack):
            query_head, keys_head, values_head = head_pack
            scores = jnp.dot(query_head, keys_head.T, preferred_element_type=jnp.float32) * score_scale
            masked = jnp.where(usable, scores, -1e+30)
            row_peak = lax.optimization_barrier(jnp.max(masked, axis=1, keepdims=True))
            weights = jnp.where(usable, jnp.exp(masked - row_peak), 0.0).astype(jnp.bfloat16)
            row_total = lax.optimization_barrier(jnp.sum(weights.astype(jnp.float32), axis=1, keepdims=True))
            mixture = jnp.dot(weights, values_head, preferred_element_type=jnp.float32)
            return mixture / row_total
        heads_out = lax.map(one_head, (query_sample.transpose(1, 0, 2), keys_sample.transpose(1, 0, 2), values_sample.transpose(1, 0, 2)))
        return heads_out.transpose(1, 0, 2).reshape(NEW, D)
    attended = lax.map(one_sample, (queries, keys_all, values_all, key_start, key_end))
    attended = attended.astype(jnp.bfloat16).reshape(SAMPLES * NEW, D)
    projected = jnp.dot(attended, w_out, preferred_element_type=jnp.float32).astype(jnp.bfloat16)
    return projected.reshape(SAMPLES, NEW, D)
```

```python
import functools
import math

import jax
import jax.numpy as jnp
from jax import lax
from jax.experimental import pallas as pl
from jax.experimental.pallas import tpu as pltpu
from jax.sharding import PartitionSpec as P

HD = 128
MESH = pl.DeviceIdType.MESH
LOW = -1e30
FLOOR = -1e29
RATE = HD ** (-0.5) * math.log2(math.e)
F32 = jnp.float32
BF16 = jnp.bfloat16


def greet(peers):
    barrier = pltpu.get_barrier_semaphore()
    for peer in peers:
        pl.semaphore_signal(barrier, inc=1, device_id=peer, device_id_type=MESH)
    pl.semaphore_wait(barrier, len(peers))


def split_parts(width):
    half = width // 2
    return (
        (0, half, True, F32),
        (half, half, False, F32),
        (width, width, True, BF16),
        (2 * width, width, False, BF16),
    )


def project_kernel(ns, nh, nk, tok, w, q_out, kv_out, *scratch):
    (tokg, wboth, xs, xr, qall, zs, zr, ws, wr, wl, as_, ar, al, qs, qr) = scratch[:15]
    rest = scratch[15:]
    s, h, k = lax.axis_index("section"), lax.axis_index("head"), lax.axis_index("kv")
    nx = ns // 2
    x, c = s // 2, lax.rem(s, 2)
    rows, width = tok.shape
    depth = w.shape[0]

    def at_x(dx):
        return lax.rem(x + dx, nx)

    def at_k(dk):
        return lax.rem(k + dk, nk)

    offsets = [(dx, dk) for dx in range(nx) for dk in range(nk)]
    z_peers = [{"head": lax.rem(h + d, nh)} for d in range(1, nh)]
    core_peer = {"section": 2 * x + 1 - c}
    plane = {o: {"section": 2 * at_x(o[0]) + c, "kv": at_k(o[1])} for o in offsets}
    greet(z_peers + [core_peer] + [plane[o] for o in offsets if o != (0, 0)])

    pending = []

    def send(src, dst, ss, rs, peer):
        copy = pltpu.make_async_remote_copy(
            src_ref=src, dst_ref=dst, send_sem=ss, recv_sem=rs, device_id=peer, device_id_type=MESH
        )
        copy.start()
        pending.append(copy)
        return copy

    z_copies = [
        send(tok, tokg.at[d], zs.at[d], zr.at[d], z_peers[d]) for d in range(nh - 1)
    ]
    w_copy = send(w, wboth.at[c], ws, wr, core_peer)
    w_local = pltpu.make_async_copy(w, wboth.at[c], wl)
    w_local.start()

    own = tok[...].astype(F32)
    squares = jnp.sum(own * own, axis=1, keepdims=True)
    for d in range(nh - 1):
        z_copies[d].wait_recv()
        part = tokg[d].astype(F32)
        squares = squares + jnp.sum(part * part, axis=1, keepdims=True)
    factor = lax.rsqrt(squares * (1.0 / (width * nh)) + 1e-05)
    per_slot = width // depth

    def place(index, values):
        section, kv = index // nk, lax.rem(index, nk)
        xs[(section // 2) * nk + kv, :, pl.ds(pl.multiple_of(lax.rem(section, 2) * depth, depth), depth)] = values

    for d in range(nh):
        block = tok[...] if d == 0 else tokg[d - 1]
        scaled = (block.astype(F32) * factor).astype(BF16)
        origin = lax.rem(h + nh - d, nh)
        for j in range(per_slot):
            place(origin * per_slot + j, scaled[:, j * depth:(j + 1) * depth])

    a_copies = []
    mine = x * nk + k
    for i, o in enumerate(offsets):
        if o == (0, 0):
            continue
        a_copies.append(
            send(xs.at[at_x(o[0]) * nk + at_k(o[1])], xr.at[mine], as_.at[i], ar.at[i], plane[o])
        )
    a_local = pltpu.make_async_copy(xs.at[mine], xr.at[mine], al)
    a_local.start()
    w_local.wait()
    w_copy.wait_recv()
    a_local.wait()
    for copy in a_copies:
        copy.wait_recv()

    parts = split_parts(width)
    hop1 = []
    per = len(rest) // len(parts)
    bufs = [rest[i * per:(i + 1) * per] for i in range(len(parts))]
    inputs = xr[...].reshape(nx * nk * rows, 2 * depth)
    for (start, cols, x_first, kind), (full, out1, in1, out2, in2, sems) in zip(parts, bufs):
        step = min(cols, 512)
        for t in range(0, cols, step):
            piece = pl.ds(start + t, step)
            total = jnp.dot(inputs[:, :depth], wboth[0, :, piece], preferred_element_type=F32)
            total = total + jnp.dot(inputs[:, depth:], wboth[1, :, piece], preferred_element_type=F32)
            full[:, :, :, t:t + step] = total.reshape(nx, nk, rows, step)
        n1, n2 = (nx, nk) if x_first else (nk, nx)
        copies = []
        for d in range(1, n1):
            if x_first:
                out1[d - 1] = full[at_x(d)].astype(kind)
                peer = plane[(d, 0)]
            else:
                for xx in range(nx):
                    out1[d - 1, xx] = full[xx, at_k(d)].astype(kind)
                peer = plane[(0, d)]
            copies.append(send(out1.at[d - 1], in1.at[d - 1], sems.at[0, d], sems.at[1, d], peer))
        hop1.append(copies)

    hop2 = []
    for (start, cols, x_first, kind), (full, out1, in1, out2, in2, sems), copies in zip(parts, bufs, hop1):
        n1, n2 = (nx, nk) if x_first else (nk, nx)
        for copy in copies:
            copy.wait_recv()
        second = []

        def summed(other):
            total = full[x, other] if x_first else full[other, k]
            for d in range(n1 - 1):
                total = total + in1[d, other].astype(F32)
            return total

        for d in range(1, n2):
            other = at_k(d) if x_first else at_x(d)
            peer = plane[(0, d)] if x_first else plane[(d, 0)]
            out2[d - 1] = summed(other).astype(kind)
            second.append(send(out2.at[d - 1], in2.at[d - 1], sems.at[2, d], sems.at[3, d], peer))
        hop2.append((summed(k if x_first else x), second))

    q_copies = []
    for i, ((start, cols, x_first, kind), (full, out1, in1, out2, in2, sems)) in enumerate(zip(parts, bufs)):
        total, second = hop2[i]
        for d, copy in enumerate(second):
            copy.wait_recv()
            total = total + in2[d].astype(F32)
        if start < width:
            qall[k, :, start:start + cols] = total.astype(BF16)
            if start + cols == width:
                for d in range(1, nk):
                    q_copies.append(
                        send(qall.at[k], qall.at[k], qs.at[d], qr.at[d], plane[(0, d)])
                    )
        else:
            kv_out[:, start - width:start - width + cols] = total.astype(BF16)
    for copy in q_copies:
        copy.wait_recv()
    for copy in pending:
        copy.wait_send()
    q_out[...] = qall[...].reshape(nk * rows, width)


def project(ns, nh, nk, tokens, weights):
    rows, width = tokens.shape
    depth = weights.shape[0]
    nx = ns // 2
    dma = pltpu.SemaphoreType.DMA
    scratch = [
        pltpu.VMEM((nh - 1, rows, width), BF16),
        pltpu.VMEM((2, depth, 3 * width), BF16),
        pltpu.VMEM((nx * nk, rows, 2 * depth), BF16),
        pltpu.VMEM((nx * nk, rows, 2 * depth), BF16),
        pltpu.VMEM((nk, rows, width), BF16),
        dma((nh - 1,)), dma((nh - 1,)), dma, dma, dma,
        dma((nx * nk,)), dma((nx * nk,)), dma,
        dma((nk,)), dma((nk,)),
    ]
    for start, cols, x_first, kind in split_parts(width):
        n1, n2 = (nx, nk) if x_first else (nk, nx)
        scratch += [
            pltpu.VMEM((nx, nk, rows, cols), F32),
            pltpu.VMEM((max(n1 - 1, 1), n2, rows, cols), kind),
            pltpu.VMEM((max(n1 - 1, 1), n2, rows, cols), kind),
            pltpu.VMEM((max(n2 - 1, 1), rows, cols), kind),
            pltpu.VMEM((max(n2 - 1, 1), rows, cols), kind),
            dma((4, max(n1, n2))),
        ]
    vmem = pl.BlockSpec(memory_space=pltpu.VMEM)
    return pl.pallas_call(
        functools.partial(project_kernel, ns, nh, nk),
        out_shape=(
            jax.ShapeDtypeStruct((nk * rows, width), BF16),
            jax.ShapeDtypeStruct((rows, 2 * width), BF16),
        ),
        in_specs=[vmem, vmem],
        out_specs=(vmem, vmem),
        scratch_shapes=scratch,
        compiler_params=pltpu.CompilerParams(
            collective_id=0, has_side_effects=True, vmem_limit_bytes=56 * 1024 * 1024
        ),
        name="project",
    )(tokens, weights)


def attend_kernel(q_ref, ck_ref, cv_ref, nk_ref, nv_ref, start_ref, end_ref, mix_ref, peak_ref, total_ref):
    part, head = pl.program_id(0), pl.program_id(1)
    kv = lax.axis_index("kv")
    block, keys, news = q_ref.shape[0], ck_ref.shape[0], nk_ref.shape[0]
    contract = (((1,), (1,)), ((), ()))
    queries = q_ref[...]
    place = kv * keys + lax.broadcasted_iota(jnp.int32, (1, keys), 1)
    bias = jnp.where((place >= start_ref[0]) & (place < end_ref[0]), 0.0, LOW)
    old = lax.dot_general(queries, ck_ref[...], contract, preferred_element_type=F32) + bias
    new = lax.dot_general(queries, nk_ref[...], contract, preferred_element_type=F32)
    new_place = kv * news + lax.broadcasted_iota(jnp.int32, (block, news), 1)
    query_place = part * block + lax.broadcasted_iota(jnp.int32, (block, news), 0)
    new = jnp.where(new_place <= query_place, new, LOW)
    peak = jnp.maximum(
        jnp.max(old, axis=1, keepdims=True), jnp.max(new, axis=1, keepdims=True)
    )
    peak = jnp.maximum(peak, FLOOR)
    old_weights = jnp.exp2((old - peak) * RATE).astype(BF16)
    new_weights = jnp.exp2((new - peak) * RATE).astype(BF16)
    total = jnp.sum(old_weights.astype(F32), axis=1, keepdims=True) + jnp.sum(
        new_weights.astype(F32), axis=1, keepdims=True
    )
    mix_ref[...] = jnp.dot(old_weights, cv_ref[...], preferred_element_type=F32) + jnp.dot(
        new_weights, nv_ref[...], preferred_element_type=F32
    )
    lane = lax.broadcasted_iota(jnp.int32, peak_ref.shape, 1)

    @pl.when(head == 0)
    def _():
        peak_ref[...] = jnp.zeros_like(peak_ref)
        total_ref[...] = jnp.zeros_like(total_ref)

    peak_ref[...] = jnp.where(lane == head, peak, peak_ref[...])
    total_ref[...] = jnp.where(lane == head, total, total_ref[...])


def attend(queries, cache_keys, cache_values, new_pair, key_start, key_end):
    count, width = queries.shape
    heads = width // HD
    keys, news = cache_keys.shape[1], new_pair.shape[0]
    block = 256 if count % 256 == 0 else count
    smem = pl.BlockSpec(memory_space=pltpu.SMEM)
    return pl.pallas_call(
        attend_kernel,
        grid=(count // block, heads),
        out_shape=(
            jax.ShapeDtypeStruct((count, width), F32),
            jax.ShapeDtypeStruct((count, HD), F32),
            jax.ShapeDtypeStruct((count, HD), F32),
        ),
        in_specs=[
            pl.BlockSpec((block, HD), lambda i, n: (i, n)),
            pl.BlockSpec((None, keys, HD), lambda i, n: (0, 0, n)),
            pl.BlockSpec((None, keys, HD), lambda i, n: (0, 0, n)),
            pl.BlockSpec((news, HD), lambda i, n: (0, n)),
            pl.BlockSpec((news, HD), lambda i, n: (0, heads + n)),
            smem,
            smem,
        ],
        out_specs=(
            pl.BlockSpec((block, HD), lambda i, n: (i, n)),
            pl.BlockSpec((block, HD), lambda i, n: (i, 0)),
            pl.BlockSpec((block, HD), lambda i, n: (i, 0)),
        ),
        compiler_params=pltpu.CompilerParams(vmem_limit_bytes=48 * 1024 * 1024),
        name="attend",
    )(queries, cache_keys, cache_values, new_pair, new_pair, key_start, key_end)


def finish_kernel(nh, nk, mix, peaks, totals, w_hbm, out, w, mixs, mixr, pr, tr, terms, got, wl, ms, mr, ps, prs, ts, trs, os, ors):
    h, k = lax.axis_index("head"), lax.axis_index("kv")
    rows, width = out.shape
    heads = width // HD
    kv_peers = [{"kv": lax.rem(k + d, nk)} for d in range(1, nk)]
    z_peers = [{"head": lax.rem(h + d, nh)} for d in range(1, nh)]
    load = pltpu.make_async_copy(w_hbm, w, wl)
    load.start()
    greet(kv_peers + z_peers)
    pending = []

    def send(src, dst, ss, rs, peer):
        copy = pltpu.make_async_remote_copy(
            src_ref=src, dst_ref=dst, send_sem=ss, recv_sem=rs, device_id=peer, device_id_type=MESH
        )
        copy.start()
        pending.append(copy)
        return copy

    arrivals = []
    for d in range(1, nk):
        theirs = pl.ds(pl.multiple_of(lax.rem(k + d, nk) * rows, rows), rows)
        mixs[d - 1] = mix[theirs].astype(BF16)
        peer = kv_peers[d - 1]
        arrivals.append(send(peaks.at[theirs], pr.at[d - 1], ps.at[d], prs.at[d], peer))
        arrivals.append(send(totals.at[theirs], tr.at[d - 1], ts.at[d], trs.at[d], peer))
        arrivals.append(send(mixs.at[d - 1], mixr.at[d - 1], ms.at[d], mr.at[d], peer))
    for copy in arrivals:
        copy.wait_recv()
    mine = pl.ds(pl.multiple_of(k * rows, rows), rows)
    own_peak, own_total = peaks[mine], totals[mine]
    highest = own_peak
    for d in range(nk - 1):
        highest = jnp.maximum(highest, pr[d])
    factors = [jnp.exp2((own_peak - highest) * RATE)]
    total = own_total * factors[0]
    for d in range(nk - 1):
        factors.append(jnp.exp2((pr[d] - highest) * RATE))
        total = total + tr[d] * factors[-1]
    columns = []
    for n in range(heads):
        cols = pl.ds(n * HD, HD)
        value = mix[mine, cols] * factors[0][:, n:n + 1]
        for d in range(nk - 1):
            value = value + mixr[d, :, cols].astype(F32) * factors[d + 1][:, n:n + 1]
        columns.append((value / total[:, n:n + 1]).astype(BF16))
    attended = jnp.concatenate(columns, axis=1)
    load.wait()
    copies = []
    for d in range(1, nh):
        target = lax.rem(h + d, nh)
        cols = pl.ds(pl.multiple_of(target * width, width), width)
        terms[d - 1] = jnp.dot(attended, w[:, cols], preferred_element_type=F32).astype(BF16)
        copies.append(send(terms.at[d - 1], got.at[d - 1], os.at[d], ors.at[d], z_peers[d - 1]))
    cols = pl.ds(pl.multiple_of(h * width, width), width)
    result = jnp.dot(attended, w[:, cols], preferred_element_type=F32)
    for d, copy in enumerate(copies):
        copy.wait_recv()
        result = result + got[d].astype(F32)
    out[...] = result.astype(BF16)
    for copy in pending:
        copy.wait_send()


def finish(nh, nk, mix, peaks, totals, w_out):
    count, width = mix.shape
    rows = count // nk
    dma = pltpu.SemaphoreType.DMA
    vmem = pl.BlockSpec(memory_space=pltpu.VMEM)
    more = max(nk - 1, 1)
    return pl.pallas_call(
        functools.partial(finish_kernel, nh, nk),
        out_shape=jax.ShapeDtypeStruct((rows, width), BF16),
        in_specs=[vmem, vmem, vmem, pl.BlockSpec(memory_space=pl.ANY)],
        out_specs=vmem,
        scratch_shapes=[
            pltpu.VMEM(w_out.shape, BF16),
            pltpu.VMEM((more, rows, width), BF16),
            pltpu.VMEM((more, rows, width), BF16),
            pltpu.VMEM((more, rows, HD), F32),
            pltpu.VMEM((more, rows, HD), F32),
            pltpu.VMEM((max(nh - 1, 1), rows, width), BF16),
            pltpu.VMEM((max(nh - 1, 1), rows, width), BF16),
            dma,
            dma((nk,)), dma((nk,)), dma((nk,)), dma((nk,)), dma((nk,)), dma((nk,)),
            dma((nh,)), dma((nh,)),
        ],
        compiler_params=pltpu.CompilerParams(
            collective_id=1, has_side_effects=True, vmem_limit_bytes=48 * 1024 * 1024
        ),
        name="finish",
    )(mix, peaks, totals, w_out)


def shards(ns, nh, nk, tokens, w_query, w_keyvalue, cache_keys, cache_values, key_start, key_end, w_out):
    weights = jnp.concatenate([w_query, w_keyvalue[:, 0, :], w_keyvalue[:, 1, :]], axis=1)
    w_full = lax.all_gather(w_out, ("section", "kv"), axis=1, tiled=True)
    queries, new_pair = project(ns, nh, nk, tokens[0], weights)
    mix, peaks, totals = attend(queries, cache_keys, cache_values, new_pair, key_start, key_end)
    return finish(nh, nk, mix, peaks, totals, w_full)[None]


def solution(mesh):
    placed = (
        P("section", "kv", "head"),
        P(("section", "kv"), "head"),
        P(("section", "kv"), None, "head"),
        P("section", "kv", "head"),
        P("section", "kv", "head"),
        P("section"),
        P("section"),
        P("head", ("section", "kv")),
    )
    body = functools.partial(shards, mesh.shape["section"], mesh.shape["head"], mesh.shape["kv"])
    return jax.shard_map(
        body, mesh=mesh, in_specs=placed, out_specs=P("section", "kv", "head"), check_vma=False
    )
```

```python
import functools
import math

import jax
import jax.numpy as jnp
from jax import lax
from jax.experimental import pallas as pl
from jax.experimental.pallas import tpu as pltpu
from jax.sharding import PartitionSpec as P

HD = 128
MESH = pl.DeviceIdType.MESH
LOW = -1e30
FLOOR = -1e29
RATE = HD ** (-0.5) * math.log2(math.e)
F32 = jnp.float32
BF16 = jnp.bfloat16


def greet(peers):
    barrier = pltpu.get_barrier_semaphore()
    for peer in peers:
        pl.semaphore_signal(barrier, inc=1, device_id=peer, device_id_type=MESH)
    pl.semaphore_wait(barrier, len(peers))


def split_parts(width):
    half = width // 2
    return (
        (0, half, True, F32),
        (half, half, False, F32),
        (width, width, True, BF16),
        (2 * width, width, False, BF16),
    )


def block_kernel(
    ns, nh, nk, tok, wq, wk, wv, ck_hbm, cv_hbm, start_ref, end_ref, out,
    tokg, wboth, xr, xn, facs, facr, qall, ck, cv, pair, mix, stat, mixs, mixr, statr,
    zs, zr, ws, wr, wl, fs, fr, gs, gr, qs, qr, cl, ms, mr, ss_, sr_, *rest
):
    s, h, k = lax.axis_index("section"), lax.axis_index("head"), lax.axis_index("kv")
    nx = ns // 2
    x, c = s // 2, lax.rem(s, 2)
    rows, width = tok.shape
    depth = wq.shape[0]
    heads = width // HD
    keys = ck.shape[0]
    mine = x * nk + k
    per_slot = width // depth

    def at_x(dx):
        return lax.rem(x + dx, nx)

    def at_k(dk):
        return lax.rem(k + dk, nk)

    offsets = [(dx, dk) for dx in range(nx) for dk in range(nk)]
    z_peers = [{"head": lax.rem(h + d, nh)} for d in range(1, nh)]
    core_peer = {"section": 2 * x + 1 - c}
    plane = {o: {"section": 2 * at_x(o[0]) + c, "kv": at_k(o[1])} for o in offsets}
    greet(z_peers + [core_peer] + [plane[o] for o in offsets if o != (0, 0)])

    pending = []

    def send(src, dst, send_sem, recv_sem, peer):
        copy = pltpu.make_async_remote_copy(
            src_ref=src, dst_ref=dst, send_sem=send_sem, recv_sem=recv_sem, device_id=peer, device_id_type=MESH
        )
        copy.start()
        pending.append(copy)
        return copy

    z_copies = [
        send(tok, tokg.at[d], zs.at[d], zr.at[d], z_peers[d]) for d in range(nh - 1)
    ]

    forwards = []

    def forward(d, block):
        origin = lax.rem(h + nh - d, nh)
        for j in range(per_slot):
            index = origin * per_slot + j
            section, kv = index // nk, lax.rem(index, nk)
            core = lax.rem(section, 2)
            src = block.at[:, pl.ds(j * depth, depth)]
            dst = xr.at[mine, core]
            here = (section // 2 == x) & (kv == k)
            far = pltpu.make_async_remote_copy(
                src_ref=src, dst_ref=dst, send_sem=gs.at[d, j], recv_sem=gr.at[mine, core],
                device_id={"section": (section // 2) * 2 + c, "kv": kv}, device_id_type=MESH,
            )
            near = pltpu.make_async_copy(src, dst, gr.at[mine, core])

            @pl.when(here)
            def _():
                near.start()

            @pl.when(jnp.logical_not(here))
            def _():
                far.start()

            forwards.append((here, far))

    forward(0, tok)
    w_copies, w_locals = [], []
    for i, w in enumerate((wq, wk, wv)):
        spot = wboth.at[c, :, pl.ds(i * width, width)]
        w_copies.append(send(w, spot, ws.at[i], wr.at[i], core_peer))
        local = pltpu.make_async_copy(w, spot, wl.at[i])
        local.start()
        w_locals.append(local)
    loads = [
        pltpu.make_async_copy(ck_hbm.at[0], ck, cl.at[0]),
        pltpu.make_async_copy(cv_hbm.at[0], cv, cl.at[1]),
    ]
    for load in loads:
        load.start()

    own = tok[...].astype(F32)
    squares = jnp.sum(own * own, axis=1, keepdims=True)
    for d in range(1, nh):
        z_copies[d - 1].wait_recv()
        forward(d, tokg.at[d - 1])
        part = tokg[d - 1].astype(F32)
        squares = squares + jnp.sum(part * part, axis=1, keepdims=True)
    factor = lax.rsqrt(squares * (1.0 / (width * nh)) + 1e-05)
    facs[...] = jnp.broadcast_to(factor, (rows, HD))
    facr[mine] = facs[...]
    f_copies = []
    for i, o in enumerate(offsets):
        if o != (0, 0):
            f_copies.append(send(facs, facr.at[mine], fs.at[i], fr.at[i], plane[o]))
    for copy in w_copies:
        copy.wait_recv()
    for copy in w_locals:
        copy.wait()
    for g in range(nx * nk):
        for core in range(2):
            pltpu.make_async_copy(xr.at[g, core], xr.at[g, core], gr.at[g, core]).wait()
    for copy in f_copies:
        copy.wait_recv()
    for g in range(nx * nk):
        scale = facr[g][:, :1]
        for core in range(2):
            xn[core, pl.ds(g * rows, rows), :] = (xr[g, core].astype(F32) * scale).astype(BF16)

    parts = split_parts(width)
    per = len(rest) // len(parts)
    bufs = [rest[i * per:(i + 1) * per] for i in range(len(parts))]

    def multiply(i):
        start, cols, x_first, kind = parts[i]
        full, out1 = bufs[i][:2]
        step = min(cols, 512)
        for t in range(0, cols, step):
            piece = pl.ds(start + t, step)
            total = jnp.dot(xn[0], wboth[0, :, piece], preferred_element_type=F32)
            total = total + jnp.dot(xn[1], wboth[1, :, piece], preferred_element_type=F32)
            full[:, :, :, t:t + step] = total.reshape(nx, nk, rows, step)
        for d in range(1, nx if x_first else nk):
            if x_first:
                out1[d - 1] = full[at_x(d)].astype(kind)
            else:
                for xx in range(nx):
                    out1[d - 1, xx] = full[xx, at_k(d)].astype(kind)

    def first_hop(i):
        x_first = parts[i][2]
        full, out1, in1, out2, in2, sems = bufs[i]
        return [
            send(out1.at[d - 1], in1.at[d - 1], sems.at[0, d], sems.at[1, d], plane[(d, 0) if x_first else (0, d)])
            for d in range(1, nx if x_first else nk)
        ]

    def second_hop(i, copies):
        start, cols, x_first, kind = parts[i]
        full, out1, in1, out2, in2, sems = bufs[i]
        n1, n2 = (nx, nk) if x_first else (nk, nx)
        for copy in copies:
            copy.wait_recv()

        def summed(other):
            total = full[x, other] if x_first else full[other, k]
            for d in range(n1 - 1):
                total = total + in1[d, other].astype(F32)
            return total

        second = []
        for d in range(1, n2):
            out2[d - 1] = summed(at_k(d) if x_first else at_x(d)).astype(kind)
            peer = plane[(0, d) if x_first else (d, 0)]
            second.append(send(out2.at[d - 1], in2.at[d - 1], sems.at[2, d], sems.at[3, d], peer))
        return summed(k if x_first else x), second

    def last(i, total, second):
        in2 = bufs[i][4]
        for d, copy in enumerate(second):
            copy.wait_recv()
            total = total + in2[d].astype(F32)
        return total.astype(BF16)

    half = width // 2
    multiply(0)
    hop_a = first_hop(0)
    multiply(1)
    hop_b = first_hop(1)
    multiply(2)
    multiply(3)
    sum_a = second_hop(0, hop_a)
    sum_b = second_hop(1, hop_b)
    qall[k, :, :half] = last(0, *sum_a)
    qall[k, :, half:] = last(1, *sum_b)
    q_copies = [
        send(qall.at[k], qall.at[k], qs.at[d], qr.at[d], plane[(0, d)]) for d in range(1, nk)
    ]
    hop_k = first_hop(2)
    hop_v = first_hop(3)
    for load in loads:
        load.wait()

    contract = (((1,), (1,)), ((), ()))
    place = k * keys + lax.broadcasted_iota(jnp.int32, (1, keys), 1)
    bias = jnp.where((place >= start_ref[0]) & (place < end_ref[0]), 0.0, LOW)
    lane = lax.broadcasted_iota(jnp.int32, (rows, HD), 1)

    def resident(block, begin, end):
        @pl.loop(begin, end)
        def _(n):
            cols = pl.ds(pl.multiple_of(n * HD, HD), HD)
            scores = lax.dot_general(
                qall[block, :, cols], ck[:, cols], contract, preferred_element_type=F32
            ) + bias
            peak = jnp.maximum(jnp.max(scores, axis=1, keepdims=True), FLOOR)
            weights = jnp.exp2((scores - peak) * RATE).astype(BF16)
            total = jnp.sum(weights.astype(F32), axis=1, keepdims=True)
            mix[block, :, cols] = jnp.dot(weights, cv[:, cols], preferred_element_type=F32)
            stat[block] = jnp.where(lane == n, peak, jnp.where(lane == n + HD // 2, total, stat[block]))

    def fresh(block, target):
        query_place = block * rows + lax.broadcasted_iota(jnp.int32, (rows, rows), 0)
        new_place = k * rows + lax.broadcasted_iota(jnp.int32, (rows, rows), 1)
        usable = new_place <= query_place
        stats = stat[block]
        merged = stats
        for n in range(heads):
            cols = pl.ds(n * HD, HD)
            scores = lax.dot_general(
                qall[block, :, cols], pair[:, cols], contract, preferred_element_type=F32
            )
            scores = jnp.where(usable, scores, LOW)
            before = stats[:, n:n + 1]
            peak = jnp.maximum(before, jnp.max(scores, axis=1, keepdims=True))
            weights = jnp.exp2((scores - peak) * RATE).astype(BF16)
            shrink = jnp.exp2((before - peak) * RATE)
            total = stats[:, n + HD // 2:n + HD // 2 + 1] * shrink + jnp.sum(
                weights.astype(F32), axis=1, keepdims=True
            )
            value = mix[block, :, cols] * shrink + jnp.dot(
                weights, pair[:, pl.ds(width + n * HD, HD)], preferred_element_type=F32
            )
            if target is None:
                mix[block, :, cols] = value
            else:
                target[:, cols] = value.astype(BF16)
            merged = jnp.where(lane == n, peak, jnp.where(lane == n + HD // 2, total, merged))
        stat[block] = merged

    stat[...] = jnp.zeros_like(stat)
    resident(k, 0, heads)
    for copy in q_copies:
        copy.wait_recv()
    for d in range(1, nk - 1):
        resident(at_k(d), 0, heads)
    if nk > 1:
        resident(at_k(nk - 1), 0, heads // 2)
    sum_k = second_hop(2, hop_k)
    sum_v = second_hop(3, hop_v)
    if nk > 1:
        resident(at_k(nk - 1), heads // 2, heads)
    pair[:, :width] = last(2, *sum_k)
    pair[:, width:] = last(3, *sum_v)
    arrivals = []
    for d in range(1, nk):
        other = at_k(d)
        fresh(other, mixs.at[d - 1])
        arrivals.append(send(stat.at[other], statr.at[d - 1], ss_.at[d], sr_.at[d], plane[(0, d)]))
        arrivals.append(send(mixs.at[d - 1], mixr.at[d - 1], ms.at[d], mr.at[d], plane[(0, d)]))
    fresh(k, None)
    for copy in arrivals:
        copy.wait_recv()

    def tops(stats):
        return stats[:, :heads]

    def sums(stats):
        return stats[:, HD // 2:HD // 2 + heads]

    own_stat = stat[k]
    highest = tops(own_stat)
    for d in range(nk - 1):
        highest = jnp.maximum(highest, tops(statr[d]))
    factors = [jnp.exp2((tops(own_stat) - highest) * RATE)]
    total = sums(own_stat) * factors[0]
    for d in range(nk - 1):
        factors.append(jnp.exp2((tops(statr[d]) - highest) * RATE))
        total = total + sums(statr[d]) * factors[-1]
    for n in range(heads):
        cols = pl.ds(n * HD, HD)
        value = mix[k, :, cols] * factors[0][:, n:n + 1]
        for d in range(nk - 1):
            value = value + mixr[d, :, cols].astype(F32) * factors[d + 1][:, n:n + 1]
        out[:, cols] = (value / total[:, n:n + 1]).astype(BF16)

    for copy in pending:
        copy.wait_send()
    for here, far in forwards:
        @pl.when(jnp.logical_not(here))
        def _():
            far.wait_send()


def attend_block(ns, nh, nk, tokens, wq, wk, wv, cache_keys, cache_values, key_start, key_end):
    rows, width = tokens.shape
    depth = wq.shape[0]
    keys = cache_keys.shape[1]
    nx = ns // 2
    group = nx * nk
    more = max(nk - 1, 1)
    dma = pltpu.SemaphoreType.DMA
    scratch = [
        pltpu.VMEM((nh - 1, rows, width), BF16),
        pltpu.VMEM((2, depth, 3 * width), BF16),
        pltpu.VMEM((group, 2, rows, depth), BF16),
        pltpu.VMEM((2, group * rows, depth), BF16),
        pltpu.VMEM((rows, HD), F32),
        pltpu.VMEM((group, rows, HD), F32),
        pltpu.VMEM((nk, rows, width), BF16),
        pltpu.VMEM((keys, width), BF16),
        pltpu.VMEM((keys, width), BF16),
        pltpu.VMEM((rows, 2 * width), BF16),
        pltpu.VMEM((nk, rows, width), F32),
        pltpu.VMEM((nk, rows, HD), F32),
        pltpu.VMEM((more, rows, width), BF16),
        pltpu.VMEM((more, rows, width), BF16),
        pltpu.VMEM((more, rows, HD), F32),
        dma((nh - 1,)), dma((nh - 1,)),
        dma((3,)), dma((3,)), dma((3,)),
        dma((group,)), dma((group,)),
        dma((nh, width // depth)), dma((group, 2)),
        dma((nk,)), dma((nk,)),
        dma((2,)),
        dma((nk,)), dma((nk,)), dma((nk,)), dma((nk,)),
    ]
    for start, cols, x_first, kind in split_parts(width):
        n1, n2 = (nx, nk) if x_first else (nk, nx)
        scratch += [
            pltpu.VMEM((nx, nk, rows, cols), F32),
            pltpu.VMEM((max(n1 - 1, 1), n2, rows, cols), kind),
            pltpu.VMEM((max(n1 - 1, 1), n2, rows, cols), kind),
            pltpu.VMEM((max(n2 - 1, 1), rows, cols), kind),
            pltpu.VMEM((max(n2 - 1, 1), rows, cols), kind),
            dma((4, max(n1, n2))),
        ]
    vmem = pl.BlockSpec(memory_space=pltpu.VMEM)
    smem = pl.BlockSpec(memory_space=pltpu.SMEM)
    hbm = pl.BlockSpec(memory_space=pl.ANY)
    return pl.pallas_call(
        functools.partial(block_kernel, ns, nh, nk),
        out_shape=jax.ShapeDtypeStruct((rows, width), BF16),
        in_specs=[vmem, hbm, hbm, hbm, hbm, hbm, smem, smem],
        out_specs=vmem,
        scratch_shapes=scratch,
        compiler_params=pltpu.CompilerParams(
            collective_id=0, has_side_effects=True, vmem_limit_bytes=60 * 1024 * 1024
        ),
        name="attend_block",
    )(tokens, wq, wk, wv, cache_keys, cache_values, key_start, key_end)


def finish_kernel(nh, attended_ref, w_hbm, out, w, terms, got, wl, os, ors):
    h = lax.axis_index("head")
    rows, width = out.shape
    z_peers = [{"head": lax.rem(h + d, nh)} for d in range(1, nh)]
    load = pltpu.make_async_copy(w_hbm, w, wl)
    load.start()
    greet(z_peers)
    attended = attended_ref[...]
    load.wait()
    copies = []
    for d in range(1, nh):
        target = lax.rem(h + d, nh)
        cols = pl.ds(pl.multiple_of(target * width, width), width)
        terms[d - 1] = jnp.dot(attended, w[:, cols], preferred_element_type=F32).astype(BF16)
        copy = pltpu.make_async_remote_copy(
            src_ref=terms.at[d - 1], dst_ref=got.at[d - 1], send_sem=os.at[d], recv_sem=ors.at[d],
            device_id=z_peers[d - 1], device_id_type=MESH,
        )
        copy.start()
        copies.append(copy)
    cols = pl.ds(pl.multiple_of(h * width, width), width)
    result = jnp.dot(attended, w[:, cols], preferred_element_type=F32)
    for d, copy in enumerate(copies):
        copy.wait_recv()
        result = result + got[d].astype(F32)
    out[...] = result.astype(BF16)
    for copy in copies:
        copy.wait_send()


def finish(nh, attended, w_out):
    rows, width = attended.shape
    dma = pltpu.SemaphoreType.DMA
    vmem = pl.BlockSpec(memory_space=pltpu.VMEM)
    return pl.pallas_call(
        functools.partial(finish_kernel, nh),
        out_shape=jax.ShapeDtypeStruct((rows, width), BF16),
        in_specs=[vmem, pl.BlockSpec(memory_space=pl.ANY)],
        out_specs=vmem,
        scratch_shapes=[
            pltpu.VMEM(w_out.shape, BF16),
            pltpu.VMEM((max(nh - 1, 1), rows, width), BF16),
            pltpu.VMEM((max(nh - 1, 1), rows, width), BF16),
            dma, dma((nh,)), dma((nh,)),
        ],
        compiler_params=pltpu.CompilerParams(
            collective_id=1, has_side_effects=True, vmem_limit_bytes=48 * 1024 * 1024
        ),
        name="finish",
    )(attended, w_out)


def shards(ns, nh, nk, tokens, w_query, w_keyvalue, cache_keys, cache_values, key_start, key_end, w_out):
    w_full = lax.all_gather(w_out, ("section", "kv"), axis=1, tiled=True)
    attended = attend_block(
        ns, nh, nk, tokens[0], w_query, w_keyvalue[:, 0, :], w_keyvalue[:, 1, :],
        cache_keys, cache_values, key_start, key_end,
    )
    return finish(nh, attended, w_full)[None]


def solution(mesh):
    placed = (
        P("section", "kv", "head"),
        P(("section", "kv"), "head"),
        P(("section", "kv"), None, "head"),
        P("section", "kv", "head"),
        P("section", "kv", "head"),
        P("section"),
        P("section"),
        P("head", ("section", "kv")),
    )
    body = functools.partial(shards, mesh.shape["section"], mesh.shape["head"], mesh.shape["kv"])
    return jax.shard_map(
        body, mesh=mesh, in_specs=placed, out_specs=P("section", "kv", "head"), check_vma=False
    )
```

```python
import functools
import math

import jax
import jax.numpy as jnp
from jax import lax
from jax.experimental import pallas as pl
from jax.experimental.pallas import tpu as pltpu
from jax.sharding import PartitionSpec as P

HD = 128
MESH = pl.DeviceIdType.MESH
LOW = -1e30
FLOOR = -1e29
RATE = HD ** (-0.5) * math.log2(math.e)
F32 = jnp.float32
BF16 = jnp.bfloat16


def greet(peers):
    barrier = pltpu.get_barrier_semaphore()
    for peer in peers:
        pl.semaphore_signal(barrier, inc=1, device_id=peer, device_id_type=MESH)
    pl.semaphore_wait(barrier, len(peers))


def split_parts(width):
    half = width // 2
    return (
        (0, half, True, F32),
        (half, half, False, F32),
        (width, width, True, BF16),
        (2 * width, width, False, BF16),
    )


def block_kernel(
    ns, nh, nk, tok, wq, wkv, w_out, ck_hbm, cv_hbm, start_ref, end_ref, out,
    wo, att, attg, town, tsend, tin, got, os, or_, ol, bs, br, ts, tr, vs, vr, tokg, wboth, xr, xn, facs, facr, qall, ck, cv, pair, mix, stat, mixs, mixr, statr,
    zs, zr, ws, wr, wl, fs, fr, gs, gr, qs, qr, cl, ms, mr, ss_, sr_, *rest
):
    s, h, k = lax.axis_index("section"), lax.axis_index("head"), lax.axis_index("kv")
    nx = ns // 2
    x, c = s // 2, lax.rem(s, 2)
    rows, width = tok.shape
    depth = wq.shape[0]
    heads = width // HD
    keys = ck.shape[0]
    mine = x * nk + k
    per_slot = width // depth

    def at_x(dx):
        return lax.rem(x + dx, nx)

    def at_k(dk):
        return lax.rem(k + dk, nk)

    offsets = [(dx, dk) for dx in range(nx) for dk in range(nk)]
    z_peers = [{"head": lax.rem(h + d, nh)} for d in range(1, nh)]
    core_peer = {"section": 2 * x + 1 - c}
    plane = {o: {"section": 2 * at_x(o[0]) + c, "kv": at_k(o[1])} for o in offsets}
    greet(z_peers + [core_peer] + [plane[o] for o in offsets if o != (0, 0)])

    pending = []

    def send(src, dst, send_sem, recv_sem, peer):
        copy = pltpu.make_async_remote_copy(
            src_ref=src, dst_ref=dst, send_sem=send_sem, recv_sem=recv_sem, device_id=peer, device_id_type=MESH
        )
        copy.start()
        pending.append(copy)
        return copy

    z_copies = [
        send(tok, tokg.at[d], zs.at[d], zr.at[d], z_peers[d]) for d in range(nh - 1)
    ]

    forwards = []

    def forward(d, block):
        origin = lax.rem(h + nh - d, nh)
        for j in range(per_slot):
            index = origin * per_slot + j
            section, kv = index // nk, lax.rem(index, nk)
            core = lax.rem(section, 2)
            src = block.at[:, pl.ds(j * depth, depth)]
            dst = xr.at[mine, core]
            here = (section // 2 == x) & (kv == k)
            far = pltpu.make_async_remote_copy(
                src_ref=src, dst_ref=dst, send_sem=gs.at[d, j], recv_sem=gr.at[mine, core],
                device_id={"section": (section // 2) * 2 + c, "kv": kv}, device_id_type=MESH,
            )
            near = pltpu.make_async_copy(src, dst, gr.at[mine, core])

            @pl.when(here)
            def _():
                near.start()

            @pl.when(jnp.logical_not(here))
            def _():
                far.start()

            forwards.append((here, far))

    forward(0, tok)
    w_copies, w_locals = [], []
    for i, (w, spot) in enumerate((
        (wq, wboth.at[c, :, pl.ds(0, width)]),
        (wkv, wboth.at[c, :, pl.ds(width, 2 * width)]),
    )):
        w_copies.append(send(w, spot, ws.at[i], wr.at[i], core_peer))
        local = pltpu.make_async_copy(w, spot, wl.at[i])
        local.start()
        w_locals.append(local)
    loads = [
        pltpu.make_async_copy(ck_hbm.at[0], ck, cl.at[0]),
        pltpu.make_async_copy(cv_hbm.at[0], cv, cl.at[1]),
    ]
    for load in loads:
        load.start()
    o_copy = send(w_out, wo.at[c], os, or_, core_peer)
    o_local = pltpu.make_async_copy(w_out, wo.at[c], ol)
    o_local.start()

    own = tok[...].astype(F32)
    squares = jnp.sum(own * own, axis=1, keepdims=True)
    for d in range(1, nh):
        z_copies[d - 1].wait_recv()
        forward(d, tokg.at[d - 1])
        part = tokg[d - 1].astype(F32)
        squares = squares + jnp.sum(part * part, axis=1, keepdims=True)
    factor = lax.rsqrt(squares * (1.0 / (width * nh)) + 1e-05)
    facs[...] = jnp.broadcast_to(factor, (rows, HD))
    facr[mine] = facs[...]
    f_copies = []
    for i, o in enumerate(offsets):
        if o != (0, 0):
            f_copies.append(send(facs, facr.at[mine], fs.at[i], fr.at[i], plane[o]))
    for copy in w_copies:
        copy.wait_recv()
    for copy in w_locals:
        copy.wait()
    for g in range(nx * nk):
        for core in range(2):
            pltpu.make_async_copy(xr.at[g, core], xr.at[g, core], gr.at[g, core]).wait()
    for copy in f_copies:
        copy.wait_recv()
    for g in range(nx * nk):
        scale = facr[g][:, :1]
        for core in range(2):
            xn[core, pl.ds(g * rows, rows), :] = (xr[g, core].astype(F32) * scale).astype(BF16)

    parts = split_parts(width)
    per = len(rest) // len(parts)
    bufs = [rest[i * per:(i + 1) * per] for i in range(len(parts))]

    def multiply(i):
        start, cols, x_first, kind = parts[i]
        full, out1 = bufs[i][:2]
        step = min(cols, 512)
        for t in range(0, cols, step):
            piece = pl.ds(start + t, step)
            total = jnp.dot(xn[0], wboth[0, :, piece], preferred_element_type=F32)
            total = total + jnp.dot(xn[1], wboth[1, :, piece], preferred_element_type=F32)
            full[:, :, :, t:t + step] = total.reshape(nx, nk, rows, step)
        for d in range(1, nx if x_first else nk):
            if x_first:
                out1[d - 1] = full[at_x(d)].astype(kind)
            else:
                for xx in range(nx):
                    out1[d - 1, xx] = full[xx, at_k(d)].astype(kind)

    def first_hop(i):
        x_first = parts[i][2]
        full, out1, in1, out2, in2, sems = bufs[i]
        return [
            send(out1.at[d - 1], in1.at[d - 1], sems.at[0, d], sems.at[1, d], plane[(d, 0) if x_first else (0, d)])
            for d in range(1, nx if x_first else nk)
        ]

    def second_hop(i, copies):
        start, cols, x_first, kind = parts[i]
        full, out1, in1, out2, in2, sems = bufs[i]
        n1, n2 = (nx, nk) if x_first else (nk, nx)
        for copy in copies:
            copy.wait_recv()

        def summed(other):
            total = full[x, other] if x_first else full[other, k]
            for d in range(n1 - 1):
                total = total + in1[d, other].astype(F32)
            return total

        second = []
        for d in range(1, n2):
            out2[d - 1] = summed(at_k(d) if x_first else at_x(d)).astype(kind)
            peer = plane[(0, d) if x_first else (d, 0)]
            second.append(send(out2.at[d - 1], in2.at[d - 1], sems.at[2, d], sems.at[3, d], peer))
        return summed(k if x_first else x), second

    def last(i, total, second):
        in2 = bufs[i][4]
        for d, copy in enumerate(second):
            copy.wait_recv()
            total = total + in2[d].astype(F32)
        return total.astype(BF16)

    half = width // 2
    multiply(0)
    hop_a = first_hop(0)
    multiply(1)
    hop_b = first_hop(1)
    multiply(2)
    multiply(3)
    sum_a = second_hop(0, hop_a)
    sum_b = second_hop(1, hop_b)
    qall[k, :, :half] = last(0, *sum_a)
    qall[k, :, half:] = last(1, *sum_b)
    q_copies = [
        send(qall.at[k], qall.at[k], qs.at[d], qr.at[d], plane[(0, d)]) for d in range(1, nk)
    ]
    hop_k = first_hop(2)
    hop_v = first_hop(3)
    for load in loads:
        load.wait()

    contract = (((1,), (1,)), ((), ()))
    place = k * keys + lax.broadcasted_iota(jnp.int32, (1, keys), 1)
    bias = jnp.where((place >= start_ref[0]) & (place < end_ref[0]), 0.0, LOW)
    lane = lax.broadcasted_iota(jnp.int32, (rows, HD), 1)

    def resident(block, begin, end):
        @pl.loop(begin, end)
        def _(n):
            cols = pl.ds(pl.multiple_of(n * HD, HD), HD)
            scores = lax.dot_general(
                qall[block, :, cols], ck[:, cols], contract, preferred_element_type=F32
            ) + bias
            peak = jnp.maximum(jnp.max(scores, axis=1, keepdims=True), FLOOR)
            weights = jnp.exp2((scores - peak) * RATE).astype(BF16)
            total = jnp.sum(weights.astype(F32), axis=1, keepdims=True)
            mix[block, :, cols] = jnp.dot(weights, cv[:, cols], preferred_element_type=F32)
            stat[block] = jnp.where(lane == n, peak, jnp.where(lane == n + HD // 2, total, stat[block]))

    def fresh(block, target):
        query_place = block * rows + lax.broadcasted_iota(jnp.int32, (rows, rows), 0)
        new_place = k * rows + lax.broadcasted_iota(jnp.int32, (rows, rows), 1)
        usable = new_place <= query_place
        stats = stat[block]
        merged = stats
        for n in range(heads):
            cols = pl.ds(n * HD, HD)
            scores = lax.dot_general(
                qall[block, :, cols], pair[:, cols], contract, preferred_element_type=F32
            )
            scores = jnp.where(usable, scores, LOW)
            before = stats[:, n:n + 1]
            peak = jnp.maximum(before, jnp.max(scores, axis=1, keepdims=True))
            weights = jnp.exp2((scores - peak) * RATE).astype(BF16)
            shrink = jnp.exp2((before - peak) * RATE)
            total = stats[:, n + HD // 2:n + HD // 2 + 1] * shrink + jnp.sum(
                weights.astype(F32), axis=1, keepdims=True
            )
            value = mix[block, :, cols] * shrink + jnp.dot(
                weights, pair[:, pl.ds(width + n * HD, HD)], preferred_element_type=F32
            )
            if target is None:
                mix[block, :, cols] = value
            else:
                target[:, cols] = value.astype(BF16)
            merged = jnp.where(lane == n, peak, jnp.where(lane == n + HD // 2, total, merged))
        stat[block] = merged

    stat[...] = jnp.zeros_like(stat)
    resident(k, 0, heads)
    for copy in q_copies:
        copy.wait_recv()
    for d in range(1, nk - 1):
        resident(at_k(d), 0, heads)
    if nk > 1:
        resident(at_k(nk - 1), 0, heads // 2)
    sum_k = second_hop(2, hop_k)
    sum_v = second_hop(3, hop_v)
    if nk > 1:
        resident(at_k(nk - 1), heads // 2, heads)
    pair[:, :width] = last(2, *sum_k)
    pair[:, width:] = last(3, *sum_v)
    arrivals = []
    for d in range(1, nk):
        other = at_k(d)
        fresh(other, mixs.at[d - 1])
        arrivals.append(send(stat.at[other], statr.at[d - 1], ss_.at[d], sr_.at[d], plane[(0, d)]))
        arrivals.append(send(mixs.at[d - 1], mixr.at[d - 1], ms.at[d], mr.at[d], plane[(0, d)]))
    fresh(k, None)
    for copy in arrivals:
        copy.wait_recv()

    def tops(stats):
        return stats[:, :heads]

    def sums(stats):
        return stats[:, HD // 2:HD // 2 + heads]

    own_stat = stat[k]
    highest = tops(own_stat)
    for d in range(nk - 1):
        highest = jnp.maximum(highest, tops(statr[d]))
    factors = [jnp.exp2((tops(own_stat) - highest) * RATE)]
    total = sums(own_stat) * factors[0]
    for d in range(nk - 1):
        factors.append(jnp.exp2((tops(statr[d]) - highest) * RATE))
        total = total + sums(statr[d]) * factors[-1]
    for n in range(heads):
        cols = pl.ds(n * HD, HD)
        value = mix[k, :, cols] * factors[0][:, n:n + 1]
        for d in range(nk - 1):
            value = value + mixr[d, :, cols].astype(F32) * factors[d + 1][:, n:n + 1]
        att[:, cols] = (value / total[:, n:n + 1]).astype(BF16)

    away = [o for o in offsets if o != (0, 0)]
    b_copies = [
        send(att, attg.at[i], bs.at[i], br.at[i], plane[o]) for i, o in enumerate(away)
    ]
    o_local.wait()
    o_copy.wait_recv()
    relays = []

    def relay(piece, i, o, core):
        index = (2 * at_x(o[0]) + core) * nk + at_k(o[1])
        target, j = index // per_slot, lax.rem(index, per_slot)
        here = target == h
        far = pltpu.make_async_remote_copy(
            src_ref=piece, dst_ref=got.at[h, j], send_sem=vs.at[i, core], recv_sem=vr.at[h, j],
            device_id={"head": target}, device_id_type=MESH,
        )
        near = pltpu.make_async_copy(piece, got.at[h, j], vr.at[h, j])

        @pl.when(here)
        def _():
            near.start()

        @pl.when(jnp.logical_not(here))
        def _():
            far.start()

        relays.append((here, far))

    for core in range(2):
        town[core] = jnp.dot(att[...], wo[core], preferred_element_type=F32).astype(BF16)
        relay(town.at[core], len(away), (0, 0), core)
    t_copies = []
    for i, o in enumerate(away):
        b_copies[i].wait_recv()
        back = plane[((nx - o[0]) % nx, (nk - o[1]) % nk)]
        for core in range(2):
            tsend[i, core] = jnp.dot(attg[i], wo[core], preferred_element_type=F32).astype(BF16)
            t_copies.append(send(tsend.at[i, core], tin.at[i, core], ts.at[i, core], tr.at[i, core], back))
    for i, o in enumerate(away):
        for core in range(2):
            t_copies[2 * i + core].wait_recv()
            relay(tin.at[i, core], i, o, core)
    for j in range(per_slot):
        total = None
        for d in range(nh):
            origin = lax.rem(h + d, nh)
            pltpu.make_async_copy(got.at[origin, j], got.at[origin, j], vr.at[origin, j]).wait()
            part = got[origin, j].astype(F32)
            total = part if total is None else total + part
        out[:, j * depth:(j + 1) * depth] = total.astype(BF16)

    for copy in pending:
        copy.wait_send()
    for here, far in forwards + relays:
        @pl.when(jnp.logical_not(here))
        def _():
            far.wait_send()


def attend_block(ns, nh, nk, tokens, wq, wkv, w_out, cache_keys, cache_values, key_start, key_end):
    rows, width = tokens.shape
    depth = wq.shape[0]
    keys = cache_keys.shape[1]
    nx = ns // 2
    group = nx * nk
    more = max(nk - 1, 1)
    dma = pltpu.SemaphoreType.DMA
    far = group - 1
    scratch = [
        pltpu.VMEM((2, width, depth), BF16),
        pltpu.VMEM((rows, width), BF16),
        pltpu.VMEM((far, rows, width), BF16),
        pltpu.VMEM((2, rows, depth), BF16),
        pltpu.VMEM((far, 2, rows, depth), BF16),
        pltpu.VMEM((far, 2, rows, depth), BF16),
        pltpu.VMEM((nh, width // depth, rows, depth), BF16),
        dma, dma, dma,
        dma((far,)), dma((far,)),
        dma((far, 2)), dma((far, 2)),
        dma((group, 2)), dma((nh, width // depth)),
        pltpu.VMEM((nh - 1, rows, width), BF16),
        pltpu.VMEM((2, depth, 3 * width), BF16),
        pltpu.VMEM((group, 2, rows, depth), BF16),
        pltpu.VMEM((2, group * rows, depth), BF16),
        pltpu.VMEM((rows, HD), F32),
        pltpu.VMEM((group, rows, HD), F32),
        pltpu.VMEM((nk, rows, width), BF16),
        pltpu.VMEM((keys, width), BF16),
        pltpu.VMEM((keys, width), BF16),
        pltpu.VMEM((rows, 2 * width), BF16),
        pltpu.VMEM((nk, rows, width), F32),
        pltpu.VMEM((nk, rows, HD), F32),
        pltpu.VMEM((more, rows, width), BF16),
        pltpu.VMEM((more, rows, width), BF16),
        pltpu.VMEM((more, rows, HD), F32),
        dma((nh - 1,)), dma((nh - 1,)),
        dma((3,)), dma((3,)), dma((3,)),
        dma((group,)), dma((group,)),
        dma((nh, width // depth)), dma((group, 2)),
        dma((nk,)), dma((nk,)),
        dma((2,)),
        dma((nk,)), dma((nk,)), dma((nk,)), dma((nk,)),
    ]
    for start, cols, x_first, kind in split_parts(width):
        n1, n2 = (nx, nk) if x_first else (nk, nx)
        scratch += [
            pltpu.VMEM((nx, nk, rows, cols), F32),
            pltpu.VMEM((max(n1 - 1, 1), n2, rows, cols), kind),
            pltpu.VMEM((max(n1 - 1, 1), n2, rows, cols), kind),
            pltpu.VMEM((max(n2 - 1, 1), rows, cols), kind),
            pltpu.VMEM((max(n2 - 1, 1), rows, cols), kind),
            dma((4, max(n1, n2))),
        ]
    vmem = pl.BlockSpec(memory_space=pltpu.VMEM)
    smem = pl.BlockSpec(memory_space=pltpu.SMEM)
    hbm = pl.BlockSpec(memory_space=pl.ANY)
    return pl.pallas_call(
        functools.partial(block_kernel, ns, nh, nk),
        out_shape=jax.ShapeDtypeStruct((rows, width), BF16),
        in_specs=[vmem, hbm, hbm, hbm, hbm, hbm, smem, smem],
        out_specs=vmem,
        scratch_shapes=scratch,
        compiler_params=pltpu.CompilerParams(
            collective_id=0, has_side_effects=True, vmem_limit_bytes=60 * 1024 * 1024
        ),
        name="attend_block",
    )(tokens, wq, wkv, w_out, cache_keys, cache_values, key_start, key_end)


def shards(ns, nh, nk, tokens, w_query, w_keyvalue, cache_keys, cache_values, key_start, key_end, w_out):
    pair_weight = w_keyvalue.reshape(w_keyvalue.shape[0], -1)
    return attend_block(
        ns, nh, nk, tokens[0], w_query, pair_weight, w_out, cache_keys, cache_values, key_start, key_end
    )[None]


def solution(mesh):
    placed = (
        P("section", "kv", "head"),
        P(("section", "kv"), "head"),
        P(("section", "kv"), None, "head"),
        P("section", "kv", "head"),
        P("section", "kv", "head"),
        P("section"),
        P("section"),
        P("head", ("section", "kv")),
    )
    body = functools.partial(shards, mesh.shape["section"], mesh.shape["head"], mesh.shape["kv"])
    return jax.shard_map(
        body, mesh=mesh, in_specs=placed, out_specs=P("section", "kv", "head"), check_vma=False
    )
```

```python
import functools
import math

import jax
import jax.numpy as jnp
from jax import lax
from jax.experimental import pallas as pl
from jax.experimental.pallas import tpu as pltpu
from jax.sharding import PartitionSpec as P

HD = 128
MESH = pl.DeviceIdType.MESH
LOW = -1e30
FLOOR = -1e29
RATE = HD ** (-0.5) * math.log2(math.e)
F32 = jnp.float32
BF16 = jnp.bfloat16


def greet(peers):
    barrier = pltpu.get_barrier_semaphore()
    for peer in peers:
        pl.semaphore_signal(barrier, inc=1, device_id=peer, device_id_type=MESH)
    pl.semaphore_wait(barrier, len(peers))


def split_parts(width):
    half = width // 2
    return (
        (0, half, True, F32),
        (half, half, False, F32),
        (width, width, True, BF16),
        (2 * width, width, False, BF16),
    )


def block_kernel(
    ns, nh, nk, tok, wq, wkv, w_out, ck_hbm, cv_hbm, start_ref, end_ref, out,
    wo, att, attg, town, tsend, tin, got, os, or_, ol, bs, br, ts, tr, vs, vr, tokr, tokl, raw, sqs, sqg, wboth, xr, xn, facs, facr, qall, ck, cv, pair, mix, stat, mixs, mixr, statr,
    zs, zr, rl, sqss, sqsr, ws, wr, wl, fs, fr, gs, gr, qs, qr, cl, ms, mr, ss_, sr_, *rest
):
    s, h, k = lax.axis_index("section"), lax.axis_index("head"), lax.axis_index("kv")
    nx = ns // 2
    x, c = s // 2, lax.rem(s, 2)
    rows, width = tok.shape
    depth = wq.shape[0]
    heads = width // HD
    keys = ck.shape[0]
    mine = x * nk + k
    per_slot = width // depth

    def at_x(dx):
        return lax.rem(x + dx, nx)

    def at_k(dk):
        return lax.rem(k + dk, nk)

    offsets = [(dx, dk) for dx in range(nx) for dk in range(nk)]
    z_peers = [{"head": lax.rem(h + d, nh)} for d in range(1, nh)]
    core_peer = {"section": 2 * x + 1 - c}
    plane = {o: {"section": 2 * at_x(o[0]) + c, "kv": at_k(o[1])} for o in offsets}
    greet(z_peers + [core_peer] + [plane[o] for o in offsets if o != (0, 0)])

    pending = []

    def send(src, dst, send_sem, recv_sem, peer):
        copy = pltpu.make_async_remote_copy(
            src_ref=src, dst_ref=dst, send_sem=send_sem, recv_sem=recv_sem, device_id=peer, device_id_type=MESH
        )
        copy.start()
        pending.append(copy)
        return copy

    eye = lax.broadcasted_iota(jnp.int32, (rows, rows), 0) == lax.broadcasted_iota(jnp.int32, (rows, rows), 1)

    def to_row(column):
        return jnp.sum(jnp.where(eye, jnp.broadcast_to(column, (rows, rows)), 0.0), axis=0, keepdims=True)

    def to_column(row):
        return jnp.sum(jnp.where(eye, jnp.broadcast_to(row, (rows, rows)), 0.0), axis=1, keepdims=True)

    line = []

    def hop(block, way, t, valid):
        store, peer, inside = (tokr, h + 1, h + 1 < nh) if way == 0 else (tokl, h - 1, h >= 1)
        go = valid & inside
        copy = pltpu.make_async_remote_copy(
            src_ref=block, dst_ref=store.at[t], send_sem=zs.at[way, t], recv_sem=zr.at[way, t],
            device_id={"head": lax.rem(peer + nh, nh)}, device_id_type=MESH,
        )

        @pl.when(go)
        def _():
            copy.start()

        line.append((go, copy))

    always = h >= 0
    raw_load = pltpu.make_async_copy(wkv, raw, rl)
    raw_load.start()
    hop(tok, 0, 0, always)
    hop(tok, 1, 0, always)
    own = tok[...].astype(F32)
    sqs[...] = jnp.broadcast_to(to_row(jnp.sum(own * own, axis=1, keepdims=True)), sqs.shape)
    sq_copies = [
        send(sqs, sqg.at[d], sqss.at[d], sqsr.at[d], z_peers[d]) for d in range(nh - 1)
    ]

    forwards = []

    def forward(slot, block, origin, valid):
        for j in range(per_slot):
            index = origin * per_slot + j
            section, kv = index // nk, lax.rem(index, nk)
            core = lax.rem(section, 2)
            src = block.at[:, pl.ds(j * depth, depth)]
            dst = xr.at[mine, core]
            here = valid & (section // 2 == x) & (kv == k)
            leave = valid & jnp.logical_not((section // 2 == x) & (kv == k))
            section = lax.rem(section, ns)
            far = pltpu.make_async_remote_copy(
                src_ref=src, dst_ref=dst, send_sem=gs.at[slot, j], recv_sem=gr.at[mine, core],
                device_id={"section": (section // 2) * 2 + c, "kv": kv}, device_id_type=MESH,
            )
            near = pltpu.make_async_copy(src, dst, gr.at[mine, core])

            @pl.when(here)
            def _():
                near.start()

            @pl.when(leave)
            def _():
                far.start()

            forwards.append((leave, far))

    forward(0, tok, h, always)
    spot = wboth.at[c, :, pl.ds(0, width)]
    w_copies = [send(wq, spot, ws.at[0], wr.at[0], core_peer)]
    w_local = pltpu.make_async_copy(wq, spot, wl)
    w_local.start()
    loads = [
        pltpu.make_async_copy(ck_hbm.at[0], ck, cl.at[0]),
        pltpu.make_async_copy(cv_hbm.at[0], cv, cl.at[1]),
    ]
    for load in loads:
        load.start()
    o_copy = send(w_out, wo.at[c], os, or_, core_peer)
    o_local = pltpu.make_async_copy(w_out, wo.at[c], ol)
    o_local.start()

    squares = sqs[:1]
    for d in range(1, nh):
        sq_copies[d - 1].wait_recv()
        squares = squares + sqg[d - 1][:1]
    facs[...] = jnp.broadcast_to(lax.rsqrt(squares * (1.0 / (width * nh)) + 1e-05), facs.shape)
    facr[mine] = facs[...]
    f_copies = []
    for i, o in enumerate(offsets):
        if o != (0, 0):
            f_copies.append(send(facs, facr.at[mine], fs.at[i], fr.at[i], plane[o]))
    for t in range(nh - 1):
        for way, store, origin, valid in (
            (0, tokr, h - t - 1, h >= t + 1), (1, tokl, h + t + 1, h + t + 1 < nh)
        ):
            @pl.when(valid)
            def _():
                pltpu.make_async_copy(store.at[t], store.at[t], zr.at[way, t]).wait()

            if t + 1 < nh - 1:
                hop(store.at[t], way, t + 1, valid)
            forward(1 + 2 * t + way, store.at[t], lax.rem(origin + nh, nh), valid)
        if t == 0:
            raw_load.wait()
            for i in range(2):
                wboth[c, :, (1 + i) * width:(2 + i) * width] = raw[:, i, :]
            spot = wboth.at[c, :, pl.ds(width, 2 * width)]
            w_copies.append(send(spot, spot, ws.at[1], wr.at[1], core_peer))
    for copy in f_copies:
        copy.wait_recv()
    for g in range(nx * nk):
        scale = to_column(facr[g][:1])
        for core in range(2):
            pltpu.make_async_copy(xr.at[g, core], xr.at[g, core], gr.at[g, core]).wait()
            xn[core, pl.ds(g * rows, rows), :] = (xr[g, core].astype(F32) * scale).astype(BF16)
    for copy in w_copies:
        copy.wait_recv()
    w_local.wait()

    parts = split_parts(width)
    per = len(rest) // len(parts)
    bufs = [rest[i * per:(i + 1) * per] for i in range(len(parts))]

    def multiply(i):
        start, cols, x_first, kind = parts[i]
        full, out1 = bufs[i][:2]
        step = min(cols, 512)
        for t in range(0, cols, step):
            piece = pl.ds(start + t, step)
            total = jnp.dot(xn[0], wboth[0, :, piece], preferred_element_type=F32)
            total = total + jnp.dot(xn[1], wboth[1, :, piece], preferred_element_type=F32)
            full[:, :, :, t:t + step] = total.reshape(nx, nk, rows, step)
        for d in range(1, nx if x_first else nk):
            if x_first:
                out1[d - 1] = full[at_x(d)].astype(kind)
            else:
                for xx in range(nx):
                    out1[d - 1, xx] = full[xx, at_k(d)].astype(kind)

    def first_hop(i):
        x_first = parts[i][2]
        full, out1, in1, out2, in2, sems = bufs[i]
        return [
            send(out1.at[d - 1], in1.at[d - 1], sems.at[0, d], sems.at[1, d], plane[(d, 0) if x_first else (0, d)])
            for d in range(1, nx if x_first else nk)
        ]

    def second_hop(i, copies):
        start, cols, x_first, kind = parts[i]
        full, out1, in1, out2, in2, sems = bufs[i]
        n1, n2 = (nx, nk) if x_first else (nk, nx)
        for copy in copies:
            copy.wait_recv()

        def summed(other):
            total = full[x, other] if x_first else full[other, k]
            for d in range(n1 - 1):
                total = total + in1[d, other].astype(F32)
            return total

        second = []
        for d in range(1, n2):
            out2[d - 1] = summed(at_k(d) if x_first else at_x(d)).astype(kind)
            peer = plane[(0, d) if x_first else (d, 0)]
            second.append(send(out2.at[d - 1], in2.at[d - 1], sems.at[2, d], sems.at[3, d], peer))
        return summed(k if x_first else x), second

    def last(i, total, second):
        in2 = bufs[i][4]
        for d, copy in enumerate(second):
            copy.wait_recv()
            total = total + in2[d].astype(F32)
        return total.astype(BF16)

    half = width // 2
    multiply(0)
    hop_a = first_hop(0)
    multiply(1)
    hop_b = first_hop(1)
    multiply(2)
    multiply(3)
    sum_a = second_hop(0, hop_a)
    sum_b = second_hop(1, hop_b)
    hop_k = first_hop(2)
    hop_v = first_hop(3)
    qall[k, :, :half] = last(0, *sum_a)
    qall[k, :, half:] = last(1, *sum_b)
    q_copies = [
        send(qall.at[k], qall.at[k], qs.at[d], qr.at[d], plane[(0, d)]) for d in range(1, nk)
    ]
    for load in loads:
        load.wait()

    contract = (((1,), (1,)), ((), ()))
    place = k * keys + lax.broadcasted_iota(jnp.int32, (1, keys), 1)
    bias = jnp.where((place >= start_ref[0]) & (place < end_ref[0]), 0.0, LOW)
    lane = lax.broadcasted_iota(jnp.int32, (rows, HD), 1)

    def resident(block, begin, end):
        @pl.loop(begin, end)
        def _(n):
            cols = pl.ds(pl.multiple_of(n * HD, HD), HD)
            scores = lax.dot_general(
                qall[block, :, cols], ck[:, cols], contract, preferred_element_type=F32
            ) + bias
            peak = jnp.maximum(jnp.max(scores, axis=1, keepdims=True), FLOOR)
            weights = jnp.exp2((scores - peak) * RATE).astype(BF16)
            total = jnp.sum(weights.astype(F32), axis=1, keepdims=True)
            mix[block, :, cols] = jnp.dot(weights, cv[:, cols], preferred_element_type=F32)
            stat[block] = jnp.where(lane == n, peak, jnp.where(lane == n + HD // 2, total, stat[block]))

    def fresh(block, target):
        query_place = block * rows + lax.broadcasted_iota(jnp.int32, (rows, rows), 0)
        new_place = k * rows + lax.broadcasted_iota(jnp.int32, (rows, rows), 1)
        usable = new_place <= query_place
        stats = stat[block]
        merged = stats
        for n in range(heads):
            cols = pl.ds(n * HD, HD)
            scores = lax.dot_general(
                qall[block, :, cols], pair[:, cols], contract, preferred_element_type=F32
            )
            scores = jnp.where(usable, scores, LOW)
            before = stats[:, n:n + 1]
            peak = jnp.maximum(before, jnp.max(scores, axis=1, keepdims=True))
            weights = jnp.exp2((scores - peak) * RATE).astype(BF16)
            shrink = jnp.exp2((before - peak) * RATE)
            total = stats[:, n + HD // 2:n + HD // 2 + 1] * shrink + jnp.sum(
                weights.astype(F32), axis=1, keepdims=True
            )
            value = mix[block, :, cols] * shrink + jnp.dot(
                weights, pair[:, pl.ds(width + n * HD, HD)], preferred_element_type=F32
            )
            if target is None:
                mix[block, :, cols] = value
            else:
                target[:, cols] = value.astype(BF16)
            merged = jnp.where(lane == n, peak, jnp.where(lane == n + HD // 2, total, merged))
        stat[block] = merged

    stat[...] = jnp.zeros_like(stat)
    resident(k, 0, heads)
    for copy in q_copies:
        copy.wait_recv()
    for d in range(1, nk - 1):
        resident(at_k(d), 0, heads)
    if nk > 1:
        resident(at_k(nk - 1), 0, heads // 2)
    sum_k = second_hop(2, hop_k)
    sum_v = second_hop(3, hop_v)
    if nk > 1:
        resident(at_k(nk - 1), heads // 2, heads)
    pair[:, :width] = last(2, *sum_k)
    pair[:, width:] = last(3, *sum_v)
    arrivals = []
    for d in range(1, nk):
        other = at_k(d)
        fresh(other, mixs.at[d - 1])
        arrivals.append(send(stat.at[other], statr.at[d - 1], ss_.at[d], sr_.at[d], plane[(0, d)]))
        arrivals.append(send(mixs.at[d - 1], mixr.at[d - 1], ms.at[d], mr.at[d], plane[(0, d)]))
    fresh(k, None)
    for copy in arrivals:
        copy.wait_recv()

    def tops(stats):
        return stats[:, :heads]

    def sums(stats):
        return stats[:, HD // 2:HD // 2 + heads]

    own_stat = stat[k]
    highest = tops(own_stat)
    for d in range(nk - 1):
        highest = jnp.maximum(highest, tops(statr[d]))
    factors = [jnp.exp2((tops(own_stat) - highest) * RATE)]
    total = sums(own_stat) * factors[0]
    for d in range(nk - 1):
        factors.append(jnp.exp2((tops(statr[d]) - highest) * RATE))
        total = total + sums(statr[d]) * factors[-1]
    for n in range(heads):
        cols = pl.ds(n * HD, HD)
        value = mix[k, :, cols] * factors[0][:, n:n + 1]
        for d in range(nk - 1):
            value = value + mixr[d, :, cols].astype(F32) * factors[d + 1][:, n:n + 1]
        att[:, cols] = (value / total[:, n:n + 1]).astype(BF16)

    away = [o for o in offsets if o != (0, 0)]
    b_copies = [
        send(att, attg.at[i], bs.at[i], br.at[i], plane[o]) for i, o in enumerate(away)
    ]
    o_local.wait()
    o_copy.wait_recv()
    relays = []

    def relay(piece, i, o, core):
        index = (2 * at_x(o[0]) + core) * nk + at_k(o[1])
        target, j = index // per_slot, lax.rem(index, per_slot)
        here = target == h
        far = pltpu.make_async_remote_copy(
            src_ref=piece, dst_ref=got.at[h, j], send_sem=vs.at[i, core], recv_sem=vr.at[h, j],
            device_id={"head": target}, device_id_type=MESH,
        )
        near = pltpu.make_async_copy(piece, got.at[h, j], vr.at[h, j])

        @pl.when(here)
        def _():
            near.start()

        @pl.when(jnp.logical_not(here))
        def _():
            far.start()

        relays.append((here, far))

    for core in range(2):
        town[core] = jnp.dot(att[...], wo[core], preferred_element_type=F32).astype(BF16)
        relay(town.at[core], len(away), (0, 0), core)
    t_copies = []
    for i, o in enumerate(away):
        b_copies[i].wait_recv()
        back = plane[((nx - o[0]) % nx, (nk - o[1]) % nk)]
        for core in range(2):
            tsend[i, core] = jnp.dot(attg[i], wo[core], preferred_element_type=F32).astype(BF16)
            t_copies.append(send(tsend.at[i, core], tin.at[i, core], ts.at[i, core], tr.at[i, core], back))
    for i, o in enumerate(away):
        for core in range(2):
            t_copies[2 * i + core].wait_recv()
            relay(tin.at[i, core], i, o, core)
    for j in range(per_slot):
        total = None
        for d in range(nh):
            origin = lax.rem(h + d, nh)
            pltpu.make_async_copy(got.at[origin, j], got.at[origin, j], vr.at[origin, j]).wait()
            part = got[origin, j].astype(F32)
            total = part if total is None else total + part
        out[:, j * depth:(j + 1) * depth] = total.astype(BF16)

    for copy in pending:
        copy.wait_send()
    for gone, copy in forwards + line:
        @pl.when(gone)
        def _():
            copy.wait_send()

    for here, far in relays:
        @pl.when(jnp.logical_not(here))
        def _():
            far.wait_send()


def attend_block(ns, nh, nk, tokens, wq, wkv, w_out, cache_keys, cache_values, key_start, key_end):
    rows, width = tokens.shape
    depth = wq.shape[0]
    keys = cache_keys.shape[1]
    nx = ns // 2
    group = nx * nk
    more = max(nk - 1, 1)
    dma = pltpu.SemaphoreType.DMA
    far = group - 1
    scratch = [
        pltpu.VMEM((2, width, depth), BF16),
        pltpu.VMEM((rows, width), BF16),
        pltpu.VMEM((far, rows, width), BF16),
        pltpu.VMEM((2, rows, depth), BF16),
        pltpu.VMEM((far, 2, rows, depth), BF16),
        pltpu.VMEM((far, 2, rows, depth), BF16),
        pltpu.VMEM((nh, width // depth, rows, depth), BF16),
        dma, dma, dma,
        dma((far,)), dma((far,)),
        dma((far, 2)), dma((far, 2)),
        dma((group, 2)), dma((nh, width // depth)),
        pltpu.VMEM((nh - 1, rows, width), BF16),
        pltpu.VMEM((nh - 1, rows, width), BF16),
        pltpu.VMEM(wkv.shape, BF16),
        pltpu.VMEM((8, rows), F32),
        pltpu.VMEM((nh - 1, 8, rows), F32),
        pltpu.VMEM((2, depth, 3 * width), BF16),
        pltpu.VMEM((group, 2, rows, depth), BF16),
        pltpu.VMEM((2, group * rows, depth), BF16),
        pltpu.VMEM((8, rows), F32),
        pltpu.VMEM((group, 8, rows), F32),
        pltpu.VMEM((nk, rows, width), BF16),
        pltpu.VMEM((keys, width), BF16),
        pltpu.VMEM((keys, width), BF16),
        pltpu.VMEM((rows, 2 * width), BF16),
        pltpu.VMEM((nk, rows, width), F32),
        pltpu.VMEM((nk, rows, HD), F32),
        pltpu.VMEM((more, rows, width), BF16),
        pltpu.VMEM((more, rows, width), BF16),
        pltpu.VMEM((more, rows, HD), F32),
        dma((2, nh - 1)), dma((2, nh - 1)), dma,
        dma((nh - 1,)), dma((nh - 1,)),
        dma((2,)), dma((2,)), dma,
        dma((group,)), dma((group,)),
        dma((2 * nh - 1, width // depth)), dma((group, 2)),
        dma((nk,)), dma((nk,)),
        dma((2,)),
        dma((nk,)), dma((nk,)), dma((nk,)), dma((nk,)),
    ]
    for start, cols, x_first, kind in split_parts(width):
        n1, n2 = (nx, nk) if x_first else (nk, nx)
        scratch += [
            pltpu.VMEM((nx, nk, rows, cols), F32),
            pltpu.VMEM((max(n1 - 1, 1), n2, rows, cols), kind),
            pltpu.VMEM((max(n1 - 1, 1), n2, rows, cols), kind),
            pltpu.VMEM((max(n2 - 1, 1), rows, cols), kind),
            pltpu.VMEM((max(n2 - 1, 1), rows, cols), kind),
            dma((4, max(n1, n2))),
        ]
    vmem = pl.BlockSpec(memory_space=pltpu.VMEM)
    smem = pl.BlockSpec(memory_space=pltpu.SMEM)
    hbm = pl.BlockSpec(memory_space=pl.ANY)
    return pl.pallas_call(
        functools.partial(block_kernel, ns, nh, nk),
        out_shape=jax.ShapeDtypeStruct((rows, width), BF16),
        in_specs=[vmem, hbm, hbm, hbm, hbm, hbm, smem, smem],
        out_specs=vmem,
        scratch_shapes=scratch,
        compiler_params=pltpu.CompilerParams(
            collective_id=0, has_side_effects=True, vmem_limit_bytes=60 * 1024 * 1024
        ),
        name="attend_block",
    )(tokens, wq, wkv, w_out, cache_keys, cache_values, key_start, key_end)


def shards(ns, nh, nk, tokens, w_query, w_keyvalue, cache_keys, cache_values, key_start, key_end, w_out):
    return attend_block(
        ns, nh, nk, tokens[0], w_query, w_keyvalue, w_out, cache_keys, cache_values, key_start, key_end
    )[None]


def solution(mesh):
    placed = (
        P("section", "kv", "head"),
        P(("section", "kv"), "head"),
        P(("section", "kv"), None, "head"),
        P("section", "kv", "head"),
        P("section", "kv", "head"),
        P("section"),
        P("section"),
        P("head", ("section", "kv")),
    )
    body = functools.partial(shards, mesh.shape["section"], mesh.shape["head"], mesh.shape["kv"])
    return jax.shard_map(
        body, mesh=mesh, in_specs=placed, out_specs=P("section", "kv", "head"), check_vma=False
    )
```

```python
import functools
import math

import jax
import jax.numpy as jnp
from jax import lax
from jax.experimental import pallas as pl
from jax.experimental.pallas import tpu as pltpu
from jax.sharding import PartitionSpec as P

HD = 128
MESH = pl.DeviceIdType.MESH
LOW = -1e30
FLOOR = -1e29
RATE = HD ** (-0.5) * math.log2(math.e)
F32 = jnp.float32
BF16 = jnp.bfloat16


def greet(peers):
    barrier = pltpu.get_barrier_semaphore()
    for peer in peers:
        pl.semaphore_signal(barrier, inc=1, device_id=peer, device_id_type=MESH)
    pl.semaphore_wait(barrier, len(peers))


def split_parts(width):
    half = width // 2
    return (
        (0, half, True, F32),
        (half, half, False, F32),
        (width, width, True, BF16),
        (2 * width, width, False, BF16),
    )


def block_kernel(
    ns, nh, nk, tok, wq, wkv, w_out, ck_hbm, cv_hbm, start_ref, end_ref, out,
    wo, att, attg, town, tsend, tin, got, os, or_, ol, bs, br, ts, tr, vs, vr, tokr, tokl, raw, sqs, sqg, wboth, xr, xn, facs, facr, qall, ck, cv, pair, mix, stat, mixs, mixr, statr,
    zs, zr, rl, sqss, sqsr, ws, wr, wl, fs, fr, gs, gr, qs, qr, cl, ms, mr, ss_, sr_, *rest
):
    s, h, k = lax.axis_index("section"), lax.axis_index("head"), lax.axis_index("kv")
    nx = ns // 2
    x, c = s // 2, lax.rem(s, 2)
    rows, width = tok.shape
    depth = wq.shape[0]
    heads = width // HD
    keys = ck.shape[0]
    mine = x * nk + k
    per_slot = width // depth

    def at_x(dx):
        return lax.rem(x + dx, nx)

    def at_k(dk):
        return lax.rem(k + dk, nk)

    offsets = [(dx, dk) for dx in range(nx) for dk in range(nk)]
    z_peers = [{"head": lax.rem(h + d, nh)} for d in range(1, nh)]
    core_peer = {"section": 2 * x + 1 - c}
    plane = {o: {"section": 2 * at_x(o[0]) + c, "kv": at_k(o[1])} for o in offsets}
    greet(z_peers + [core_peer] + [plane[o] for o in offsets if o != (0, 0)])

    pending = []

    def send(src, dst, send_sem, recv_sem, peer):
        copy = pltpu.make_async_remote_copy(
            src_ref=src, dst_ref=dst, send_sem=send_sem, recv_sem=recv_sem, device_id=peer, device_id_type=MESH
        )
        copy.start()
        pending.append(copy)
        return copy

    eye = lax.broadcasted_iota(jnp.int32, (rows, rows), 0) == lax.broadcasted_iota(jnp.int32, (rows, rows), 1)

    def to_row(column):
        return jnp.sum(jnp.where(eye, jnp.broadcast_to(column, (rows, rows)), 0.0), axis=0, keepdims=True)

    def to_column(row):
        return jnp.sum(jnp.where(eye, jnp.broadcast_to(row, (rows, rows)), 0.0), axis=1, keepdims=True)

    line = []

    def hop(block, way, t, j, valid):
        store, peer, inside = (tokr, h + 1, h + 1 < nh) if way == 0 else (tokl, h - 1, h >= 1)
        go = valid & inside
        copy = pltpu.make_async_remote_copy(
            src_ref=block.at[:, pl.ds(j * depth, depth)], dst_ref=store.at[t, :, pl.ds(j * depth, depth)],
            send_sem=zs.at[way, t, j], recv_sem=zr.at[way, t, j],
            device_id={"head": lax.rem(peer + nh, nh)}, device_id_type=MESH,
        )

        @pl.when(go)
        def _():
            copy.start()

        line.append((go, copy))

    always = h >= 0
    raw_load = pltpu.make_async_copy(wkv, raw, rl)
    raw_load.start()
    for j in range(per_slot):
        hop(tok, 0, 0, j, always)
        hop(tok, 1, 0, j, always)
    own = tok[...].astype(F32)
    sqs[...] = jnp.broadcast_to(to_row(jnp.sum(own * own, axis=1, keepdims=True)), sqs.shape)
    sq_copies = [
        send(sqs, sqg.at[d], sqss.at[d], sqsr.at[d], z_peers[d]) for d in range(nh - 1)
    ]

    forwards = []

    def forward(slot, block, origin, pieces, valid):
        for j in pieces:
            index = origin * per_slot + j
            section, kv = index // nk, lax.rem(index, nk)
            core = lax.rem(section, 2)
            src = block.at[:, pl.ds(j * depth, depth)]
            dst = xr.at[mine, core]
            here = valid & (section // 2 == x) & (kv == k)
            leave = valid & jnp.logical_not((section // 2 == x) & (kv == k))
            section = lax.rem(section, ns)
            far = pltpu.make_async_remote_copy(
                src_ref=src, dst_ref=dst, send_sem=gs.at[slot, j], recv_sem=gr.at[mine, core],
                device_id={"section": (section // 2) * 2 + c, "kv": kv}, device_id_type=MESH,
            )
            near = pltpu.make_async_copy(src, dst, gr.at[mine, core])

            @pl.when(here)
            def _():
                near.start()

            @pl.when(leave)
            def _():
                far.start()

            forwards.append((leave, far))

    forward(0, tok, h, range(per_slot), always)
    spot = wboth.at[c, :, pl.ds(0, width)]
    w_copies = [send(wq, spot, ws.at[0], wr.at[0], core_peer)]
    w_local = pltpu.make_async_copy(wq, spot, wl)
    w_local.start()
    loads = [
        pltpu.make_async_copy(ck_hbm.at[0], ck, cl.at[0]),
        pltpu.make_async_copy(cv_hbm.at[0], cv, cl.at[1]),
    ]
    for load in loads:
        load.start()
    o_copy = send(w_out, wo.at[c], os, or_, core_peer)
    o_local = pltpu.make_async_copy(w_out, wo.at[c], ol)
    o_local.start()

    squares = sqs[:1]
    for d in range(1, nh):
        sq_copies[d - 1].wait_recv()
        squares = squares + sqg[d - 1][:1]
    facs[...] = jnp.broadcast_to(lax.rsqrt(squares * (1.0 / (width * nh)) + 1e-05), facs.shape)
    facr[mine] = facs[...]
    f_copies = []
    for i, o in enumerate(offsets):
        if o != (0, 0):
            f_copies.append(send(facs, facr.at[mine], fs.at[i], fr.at[i], plane[o]))
    for t in range(nh - 1):
        for j in range(per_slot):
            for way, store, origin, valid in (
                (0, tokr, h - t - 1, h >= t + 1), (1, tokl, h + t + 1, h + t + 1 < nh)
            ):
                piece = store.at[t, :, pl.ds(j * depth, depth)]

                @pl.when(valid)
                def _():
                    pltpu.make_async_copy(piece, piece, zr.at[way, t, j]).wait()

                if t + 1 < nh - 1:
                    hop(store.at[t], way, t + 1, j, valid)
                forward(1 + 2 * t + way, store.at[t], lax.rem(origin + nh, nh), (j,), valid)
        if t == 0:
            raw_load.wait()
            for i in range(2):
                wboth[c, :, (1 + i) * width:(2 + i) * width] = raw[:, i, :]
            spot = wboth.at[c, :, pl.ds(width, 2 * width)]
            w_copies.append(send(spot, spot, ws.at[1], wr.at[1], core_peer))
    for copy in f_copies:
        copy.wait_recv()
    for g in range(nx * nk):
        scale = to_column(facr[g][:1])
        for core in range(2):
            pltpu.make_async_copy(xr.at[g, core], xr.at[g, core], gr.at[g, core]).wait()
            xn[core, pl.ds(g * rows, rows), :] = (xr[g, core].astype(F32) * scale).astype(BF16)
    for copy in w_copies:
        copy.wait_recv()
    w_local.wait()

    parts = split_parts(width)
    per = len(rest) // len(parts)
    bufs = [rest[i * per:(i + 1) * per] for i in range(len(parts))]

    def multiply(i):
        start, cols, x_first, kind = parts[i]
        full, out1 = bufs[i][:2]
        step = min(cols, 512)
        for t in range(0, cols, step):
            piece = pl.ds(start + t, step)
            total = jnp.dot(xn[0], wboth[0, :, piece], preferred_element_type=F32)
            total = total + jnp.dot(xn[1], wboth[1, :, piece], preferred_element_type=F32)
            full[:, :, :, t:t + step] = total.reshape(nx, nk, rows, step)
        for d in range(1, nx if x_first else nk):
            if x_first:
                out1[d - 1] = full[at_x(d)].astype(kind)
            else:
                for xx in range(nx):
                    out1[d - 1, xx] = full[xx, at_k(d)].astype(kind)

    def first_hop(i):
        x_first = parts[i][2]
        full, out1, in1, out2, in2, sems = bufs[i]
        return [
            send(out1.at[d - 1], in1.at[d - 1], sems.at[0, d], sems.at[1, d], plane[(d, 0) if x_first else (0, d)])
            for d in range(1, nx if x_first else nk)
        ]

    def second_hop(i, copies):
        start, cols, x_first, kind = parts[i]
        full, out1, in1, out2, in2, sems = bufs[i]
        n1, n2 = (nx, nk) if x_first else (nk, nx)
        for copy in copies:
            copy.wait_recv()

        def summed(other):
            total = full[x, other] if x_first else full[other, k]
            for d in range(n1 - 1):
                total = total + in1[d, other].astype(F32)
            return total

        second = []
        for d in range(1, n2):
            out2[d - 1] = summed(at_k(d) if x_first else at_x(d)).astype(kind)
            peer = plane[(0, d) if x_first else (d, 0)]
            second.append(send(out2.at[d - 1], in2.at[d - 1], sems.at[2, d], sems.at[3, d], peer))
        return summed(k if x_first else x), second

    def last(i, total, second):
        in2 = bufs[i][4]
        for d, copy in enumerate(second):
            copy.wait_recv()
            total = total + in2[d].astype(F32)
        return total.astype(BF16)

    half = width // 2
    multiply(0)
    hop_a = first_hop(0)
    multiply(1)
    hop_b = first_hop(1)
    multiply(2)
    multiply(3)
    sum_a = second_hop(0, hop_a)
    sum_b = second_hop(1, hop_b)
    hop_k = first_hop(2)
    hop_v = first_hop(3)
    qall[k, :, :half] = last(0, *sum_a)
    qall[k, :, half:] = last(1, *sum_b)
    q_copies = [
        send(qall.at[k], qall.at[k], qs.at[d], qr.at[d], plane[(0, d)]) for d in range(1, nk)
    ]
    for load in loads:
        load.wait()

    contract = (((1,), (1,)), ((), ()))
    place = k * keys + lax.broadcasted_iota(jnp.int32, (1, keys), 1)
    bias = jnp.where((place >= start_ref[0]) & (place < end_ref[0]), 0.0, LOW)
    lane = lax.broadcasted_iota(jnp.int32, (rows, HD), 1)

    def resident(block, begin, end):
        together = 2 if (end - begin) % 2 == 0 else 1

        @pl.loop(0, (end - begin) // together)
        def _(step):
            first = begin + step * together
            columns = [
                pl.ds(pl.multiple_of((first + m) * HD, HD), HD) for m in range(together)
            ]
            scores = [
                lax.dot_general(
                    qall[block, :, cols], ck[:, cols], contract, preferred_element_type=F32
                ) + bias
                for cols in columns
            ]
            peaks = [jnp.maximum(jnp.max(each, axis=1, keepdims=True), FLOOR) for each in scores]
            stats = stat[block]
            for m, cols in enumerate(columns):
                weights = jnp.exp2((scores[m] - peaks[m]) * RATE).astype(BF16)
                total = jnp.sum(weights.astype(F32), axis=1, keepdims=True)
                mix[block, :, cols] = jnp.dot(weights, cv[:, cols], preferred_element_type=F32)
                n = first + m
                stats = jnp.where(lane == n, peaks[m], jnp.where(lane == n + HD // 2, total, stats))
            stat[block] = stats

    def fresh(block, target):
        query_place = block * rows + lax.broadcasted_iota(jnp.int32, (rows, rows), 0)
        new_place = k * rows + lax.broadcasted_iota(jnp.int32, (rows, rows), 1)
        usable = new_place <= query_place
        stats = stat[block]
        merged = stats
        for n in range(heads):
            cols = pl.ds(n * HD, HD)
            scores = lax.dot_general(
                qall[block, :, cols], pair[:, cols], contract, preferred_element_type=F32
            )
            scores = jnp.where(usable, scores, LOW)
            before = stats[:, n:n + 1]
            peak = jnp.maximum(before, jnp.max(scores, axis=1, keepdims=True))
            weights = jnp.exp2((scores - peak) * RATE).astype(BF16)
            shrink = jnp.exp2((before - peak) * RATE)
            total = stats[:, n + HD // 2:n + HD // 2 + 1] * shrink + jnp.sum(
                weights.astype(F32), axis=1, keepdims=True
            )
            value = mix[block, :, cols] * shrink + jnp.dot(
                weights, pair[:, pl.ds(width + n * HD, HD)], preferred_element_type=F32
            )
            if target is None:
                mix[block, :, cols] = value
            else:
                target[:, cols] = value.astype(BF16)
            merged = jnp.where(lane == n, peak, jnp.where(lane == n + HD // 2, total, merged))
        stat[block] = merged

    stat[...] = jnp.zeros_like(stat)
    resident(k, 0, heads)
    for copy in q_copies:
        copy.wait_recv()
    for d in range(1, nk - 1):
        resident(at_k(d), 0, heads)
    if nk > 1:
        resident(at_k(nk - 1), 0, heads // 2)
    sum_k = second_hop(2, hop_k)
    sum_v = second_hop(3, hop_v)
    if nk > 1:
        resident(at_k(nk - 1), heads // 2, heads)
    pair[:, :width] = last(2, *sum_k)
    pair[:, width:] = last(3, *sum_v)
    part_rows = rows // 2
    spans = [pl.ds(r * part_rows, part_rows) for r in range(2)]
    arrivals, mix_copies = [], []
    for d in range(1, nk):
        other = at_k(d)
        fresh(other, mixs.at[d - 1])
        arrivals.append(send(stat.at[other], statr.at[d - 1], ss_.at[d], sr_.at[d], plane[(0, d)]))
        for r, span in enumerate(spans):
            mix_copies.append(send(
                mixs.at[d - 1, span], mixr.at[d - 1, span], ms.at[d, r], mr.at[d, r], plane[(0, d)]
            ))
    fresh(k, None)
    for copy in arrivals:
        copy.wait_recv()

    def tops(stats):
        return stats[:, :heads]

    def sums(stats):
        return stats[:, HD // 2:HD // 2 + heads]

    own_stat = stat[k]
    highest = tops(own_stat)
    for d in range(nk - 1):
        highest = jnp.maximum(highest, tops(statr[d]))
    factors = [jnp.exp2((tops(own_stat) - highest) * RATE)]
    total = sums(own_stat) * factors[0]
    for d in range(nk - 1):
        factors.append(jnp.exp2((tops(statr[d]) - highest) * RATE))
        total = total + sums(statr[d]) * factors[-1]
    away = [o for o in offsets if o != (0, 0)]
    b_copies = []
    for r, span in enumerate(spans):
        for d in range(nk - 1):
            mix_copies[2 * d + r].wait_recv()
        low, high = r * part_rows, (r + 1) * part_rows
        for n in range(heads):
            cols = pl.ds(n * HD, HD)
            value = mix[k, span, cols] * factors[0][low:high, n:n + 1]
            for d in range(nk - 1):
                value = value + mixr[d, span, cols].astype(F32) * factors[d + 1][low:high, n:n + 1]
            att[span, cols] = (value / total[low:high, n:n + 1]).astype(BF16)
        b_copies.append([
            send(att.at[span], attg.at[i, span], bs.at[i, r], br.at[i, r], plane[o]) for i, o in enumerate(away)
        ])
    o_local.wait()
    o_copy.wait_recv()
    relays = []

    def relay(piece, i, o, core, r):
        index = (2 * at_x(o[0]) + core) * nk + at_k(o[1])
        target, j = index // per_slot, lax.rem(index, per_slot)
        here = target == h
        far = pltpu.make_async_remote_copy(
            src_ref=piece, dst_ref=got.at[h, j, r], send_sem=vs.at[i, core, r], recv_sem=vr.at[h, j, r],
            device_id={"head": target}, device_id_type=MESH,
        )
        near = pltpu.make_async_copy(piece, got.at[h, j, r], vr.at[h, j, r])

        @pl.when(here)
        def _():
            near.start()

        @pl.when(jnp.logical_not(here))
        def _():
            far.start()

        relays.append((here, far))

    for r, span in enumerate(spans):
        for core in range(2):
            town[core, span] = jnp.dot(att[span], wo[core], preferred_element_type=F32).astype(BF16)
            relay(town.at[core, span], len(away), (0, 0), core, r)
    t_copies = {}
    for r, span in enumerate(spans):
        for i, o in enumerate(away):
            b_copies[r][i].wait_recv()
            back = plane[((nx - o[0]) % nx, (nk - o[1]) % nk)]
            for core in range(2):
                tsend[i, core, span] = jnp.dot(attg[i, span], wo[core], preferred_element_type=F32).astype(BF16)
                t_copies[r, i, core] = send(
                    tsend.at[i, core, span], tin.at[i, core, span], ts.at[i, core, r], tr.at[i, core, r], back
                )
    for r, span in enumerate(spans):
        for i, o in enumerate(away):
            for core in range(2):
                t_copies[r, i, core].wait_recv()
                relay(tin.at[i, core, span], i, o, core, r)
    for r, span in enumerate(spans):
        for j in range(per_slot):
            total = None
            for d in range(nh):
                origin = lax.rem(h + d, nh)
                pltpu.make_async_copy(got.at[origin, j, r], got.at[origin, j, r], vr.at[origin, j, r]).wait()
                part = got[origin, j, r].astype(F32)
                total = part if total is None else total + part
            out[span, j * depth:(j + 1) * depth] = total.astype(BF16)

    for copy in pending:
        copy.wait_send()
    for gone, copy in forwards + line:
        @pl.when(gone)
        def _():
            copy.wait_send()

    for here, far in relays:
        @pl.when(jnp.logical_not(here))
        def _():
            far.wait_send()


def attend_block(ns, nh, nk, tokens, wq, wkv, w_out, cache_keys, cache_values, key_start, key_end):
    rows, width = tokens.shape
    depth = wq.shape[0]
    keys = cache_keys.shape[1]
    nx = ns // 2
    group = nx * nk
    more = max(nk - 1, 1)
    dma = pltpu.SemaphoreType.DMA
    far = group - 1
    scratch = [
        pltpu.VMEM((2, width, depth), BF16),
        pltpu.VMEM((rows, width), BF16),
        pltpu.VMEM((far, rows, width), BF16),
        pltpu.VMEM((2, rows, depth), BF16),
        pltpu.VMEM((far, 2, rows, depth), BF16),
        pltpu.VMEM((far, 2, rows, depth), BF16),
        pltpu.VMEM((nh, width // depth, 2, rows // 2, depth), BF16),
        dma, dma, dma,
        dma((far, 2)), dma((far, 2)),
        dma((far, 2, 2)), dma((far, 2, 2)),
        dma((group, 2, 2)), dma((nh, width // depth, 2)),
        pltpu.VMEM((nh - 1, rows, width), BF16),
        pltpu.VMEM((nh - 1, rows, width), BF16),
        pltpu.VMEM(wkv.shape, BF16),
        pltpu.VMEM((8, rows), F32),
        pltpu.VMEM((nh - 1, 8, rows), F32),
        pltpu.VMEM((2, depth, 3 * width), BF16),
        pltpu.VMEM((group, 2, rows, depth), BF16),
        pltpu.VMEM((2, group * rows, depth), BF16),
        pltpu.VMEM((8, rows), F32),
        pltpu.VMEM((group, 8, rows), F32),
        pltpu.VMEM((nk, rows, width), BF16),
        pltpu.VMEM((keys, width), BF16),
        pltpu.VMEM((keys, width), BF16),
        pltpu.VMEM((rows, 2 * width), BF16),
        pltpu.VMEM((nk, rows, width), F32),
        pltpu.VMEM((nk, rows, HD), F32),
        pltpu.VMEM((more, rows, width), BF16),
        pltpu.VMEM((more, rows, width), BF16),
        pltpu.VMEM((more, rows, HD), F32),
        dma((2, nh - 1, width // depth)), dma((2, nh - 1, width // depth)), dma,
        dma((nh - 1,)), dma((nh - 1,)),
        dma((2,)), dma((2,)), dma,
        dma((group,)), dma((group,)),
        dma((2 * nh - 1, width // depth)), dma((group, 2)),
        dma((nk,)), dma((nk,)),
        dma((2,)),
        dma((nk, 2)), dma((nk, 2)), dma((nk,)), dma((nk,)),
    ]
    for start, cols, x_first, kind in split_parts(width):
        n1, n2 = (nx, nk) if x_first else (nk, nx)
        scratch += [
            pltpu.VMEM((nx, nk, rows, cols), F32),
            pltpu.VMEM((max(n1 - 1, 1), n2, rows, cols), kind),
            pltpu.VMEM((max(n1 - 1, 1), n2, rows, cols), kind),
            pltpu.VMEM((max(n2 - 1, 1), rows, cols), kind),
            pltpu.VMEM((max(n2 - 1, 1), rows, cols), kind),
            dma((4, max(n1, n2))),
        ]
    vmem = pl.BlockSpec(memory_space=pltpu.VMEM)
    smem = pl.BlockSpec(memory_space=pltpu.SMEM)
    hbm = pl.BlockSpec(memory_space=pl.ANY)
    return pl.pallas_call(
        functools.partial(block_kernel, ns, nh, nk),
        out_shape=jax.ShapeDtypeStruct((rows, width), BF16),
        in_specs=[vmem, hbm, hbm, hbm, hbm, hbm, smem, smem],
        out_specs=vmem,
        scratch_shapes=scratch,
        compiler_params=pltpu.CompilerParams(
            collective_id=0, has_side_effects=True, vmem_limit_bytes=60 * 1024 * 1024
        ),
        name="attend_block",
    )(tokens, wq, wkv, w_out, cache_keys, cache_values, key_start, key_end)


def shards(ns, nh, nk, tokens, w_query, w_keyvalue, cache_keys, cache_values, key_start, key_end, w_out):
    return attend_block(
        ns, nh, nk, tokens[0], w_query, w_keyvalue, w_out, cache_keys, cache_values, key_start, key_end
    )[None]


def solution(mesh):
    placed = (
        P("section", "kv", "head"),
        P(("section", "kv"), "head"),
        P(("section", "kv"), None, "head"),
        P("section", "kv", "head"),
        P("section", "kv", "head"),
        P("section"),
        P("section"),
        P("head", ("section", "kv")),
    )
    body = functools.partial(shards, mesh.shape["section"], mesh.shape["head"], mesh.shape["kv"])
    return jax.shard_map(
        body, mesh=mesh, in_specs=placed, out_specs=P("section", "kv", "head"), check_vma=False
    )
```

```python
import functools
import math

import jax
import jax.numpy as jnp
from jax import lax
from jax.experimental import pallas as pl
from jax.experimental.pallas import tpu as pltpu
from jax.sharding import PartitionSpec as P

HD = 128
MESH = pl.DeviceIdType.MESH
LOW = -1e30
FLOOR = -1e29
RATE = HD ** (-0.5) * math.log2(math.e)
F32 = jnp.float32
BF16 = jnp.bfloat16


def greet(peers):
    barrier = pltpu.get_barrier_semaphore()
    for peer in peers:
        pl.semaphore_signal(barrier, inc=1, device_id=peer, device_id_type=MESH)
    pl.semaphore_wait(barrier, len(peers))


def split_parts(width):
    half = width // 2
    return (
        (0, half, True, F32),
        (half, half, False, F32),
        (width, width, True, BF16),
        (2 * width, width, False, BF16),
    )


def block_kernel(
    ns, nh, nk, tok, wq, wkv, w_out, ck_hbm, cv_hbm, start_ref, end_ref, out,
    wo, att, attg, town, tsend, tin, got, os, or_, ol, bs, br, ts, tr, vs, vr, tokr, tokl, raw, sqs, sqg, wboth, xr, xn, facs, facr, qall, ck, cv, pair, mix, stat, mixs, mixr, statr,
    zs, zr, rl, sqss, sqsr, ws, wr, wl, fs, fr, gs, gr, qs, qr, cl, ms, mr, ss_, sr_, *rest
):
    s, h, k = lax.axis_index("section"), lax.axis_index("head"), lax.axis_index("kv")
    nx = ns // 2
    x, c = s // 2, lax.rem(s, 2)
    rows, width = tok.shape
    depth = wq.shape[0]
    heads = width // HD
    keys = ck.shape[0]
    mine = x * nk + k
    per_slot = width // depth

    def at_x(dx):
        return lax.rem(x + dx, nx)

    def at_k(dk):
        return lax.rem(k + dk, nk)

    offsets = [(dx, dk) for dx in range(nx) for dk in range(nk)]
    z_peers = [{"head": lax.rem(h + d, nh)} for d in range(1, nh)]
    core_peer = {"section": 2 * x + 1 - c}
    plane = {o: {"section": 2 * at_x(o[0]) + c, "kv": at_k(o[1])} for o in offsets}
    greet(z_peers + [core_peer] + [plane[o] for o in offsets if o != (0, 0)])

    pending = []

    def send(src, dst, send_sem, recv_sem, peer):
        copy = pltpu.make_async_remote_copy(
            src_ref=src, dst_ref=dst, send_sem=send_sem, recv_sem=recv_sem, device_id=peer, device_id_type=MESH
        )
        copy.start()
        pending.append(copy)
        return copy

    eye = lax.broadcasted_iota(jnp.int32, (rows, rows), 0) == lax.broadcasted_iota(jnp.int32, (rows, rows), 1)

    def to_row(column):
        return jnp.sum(jnp.where(eye, jnp.broadcast_to(column, (rows, rows)), 0.0), axis=0, keepdims=True)

    def to_column(row):
        return jnp.sum(jnp.where(eye, jnp.broadcast_to(row, (rows, rows)), 0.0), axis=1, keepdims=True)

    line = []

    def hop(block, way, t, j, valid):
        store, peer, inside = (tokr, h + 1, h + 1 < nh) if way == 0 else (tokl, h - 1, h >= 1)
        go = valid & inside
        copy = pltpu.make_async_remote_copy(
            src_ref=block.at[:, pl.ds(j * depth, depth)], dst_ref=store.at[t, :, pl.ds(j * depth, depth)],
            send_sem=zs.at[way, t, j], recv_sem=zr.at[way, t, j],
            device_id={"head": lax.rem(peer + nh, nh)}, device_id_type=MESH,
        )

        @pl.when(go)
        def _():
            copy.start()

        line.append((go, copy))

    always = h >= 0
    raw_load = pltpu.make_async_copy(wkv, raw, rl)
    raw_load.start()
    for j in range(per_slot):
        hop(tok, 0, 0, j, always)
        hop(tok, 1, 0, j, always)
    own = tok[...].astype(F32)
    sqs[...] = jnp.broadcast_to(to_row(jnp.sum(own * own, axis=1, keepdims=True)), sqs.shape)
    sq_copies = [
        send(sqs, sqg.at[d], sqss.at[d], sqsr.at[d], z_peers[d]) for d in range(nh - 1)
    ]

    forwards = []

    def forward(slot, block, origin, pieces, valid):
        for j in pieces:
            index = origin * per_slot + j
            section, kv = index // nk, lax.rem(index, nk)
            core = lax.rem(section, 2)
            src = block.at[:, pl.ds(j * depth, depth)]
            dst = xr.at[mine, core]
            here = valid & (section // 2 == x) & (kv == k)
            leave = valid & jnp.logical_not((section // 2 == x) & (kv == k))
            section = lax.rem(section, ns)
            far = pltpu.make_async_remote_copy(
                src_ref=src, dst_ref=dst, send_sem=gs.at[slot, j], recv_sem=gr.at[mine, core],
                device_id={"section": (section // 2) * 2 + c, "kv": kv}, device_id_type=MESH,
            )
            near = pltpu.make_async_copy(src, dst, gr.at[mine, core])

            @pl.when(here)
            def _():
                near.start()

            @pl.when(leave)
            def _():
                far.start()

            forwards.append((leave, far))

    forward(0, tok, h, range(per_slot), always)
    spot = wboth.at[c, :, pl.ds(0, width)]
    w_copies = [send(wq, spot, ws.at[0], wr.at[0], core_peer)]
    w_local = pltpu.make_async_copy(wq, spot, wl)
    w_local.start()
    loads = [
        pltpu.make_async_copy(ck_hbm.at[0], ck, cl.at[0]),
        pltpu.make_async_copy(cv_hbm.at[0], cv, cl.at[1]),
    ]
    for load in loads:
        load.start()
    o_copy = send(w_out, wo.at[c], os, or_, core_peer)
    o_local = pltpu.make_async_copy(w_out, wo.at[c], ol)
    o_local.start()

    squares = sqs[:1]
    for d in range(1, nh):
        sq_copies[d - 1].wait_recv()
        squares = squares + sqg[d - 1][:1]
    facs[...] = jnp.broadcast_to(lax.rsqrt(squares * (1.0 / (width * nh)) + 1e-05), facs.shape)
    facr[mine] = facs[...]
    f_copies = []
    for i, o in enumerate(offsets):
        if o != (0, 0):
            f_copies.append(send(facs, facr.at[mine], fs.at[i], fr.at[i], plane[o]))
    for t in range(nh - 1):
        for j in range(per_slot):
            for way, store, origin, valid in (
                (0, tokr, h - t - 1, h >= t + 1), (1, tokl, h + t + 1, h + t + 1 < nh)
            ):
                piece = store.at[t, :, pl.ds(j * depth, depth)]

                @pl.when(valid)
                def _():
                    pltpu.make_async_copy(piece, piece, zr.at[way, t, j]).wait()

                if t + 1 < nh - 1:
                    hop(store.at[t], way, t + 1, j, valid)
                forward(1 + 2 * t + way, store.at[t], lax.rem(origin + nh, nh), (j,), valid)
        if t == 0:
            raw_load.wait()
            for i in range(2):
                wboth[c, :, (1 + i) * width:(2 + i) * width] = raw[:, i, :]
            spot = wboth.at[c, :, pl.ds(width, 2 * width)]
            w_copies.append(send(spot, spot, ws.at[1], wr.at[1], core_peer))
    for copy in f_copies:
        copy.wait_recv()
    for g in range(nx * nk):
        scale = to_column(facr[g][:1])
        for core in range(2):
            pltpu.make_async_copy(xr.at[g, core], xr.at[g, core], gr.at[g, core]).wait()
            xn[core, pl.ds(g * rows, rows), :] = (xr[g, core].astype(F32) * scale).astype(BF16)
    for copy in w_copies:
        copy.wait_recv()
    w_local.wait()

    parts = split_parts(width)
    per = len(rest) // len(parts)
    bufs = [rest[i * per:(i + 1) * per] for i in range(len(parts))]

    def multiply(i):
        start, cols, x_first, kind = parts[i]
        full, out1 = bufs[i][:2]
        step = min(cols, 512)
        for t in range(0, cols, step):
            piece = pl.ds(start + t, step)
            total = jnp.dot(xn[0], wboth[0, :, piece], preferred_element_type=F32)
            total = total + jnp.dot(xn[1], wboth[1, :, piece], preferred_element_type=F32)
            full[:, :, :, t:t + step] = total.reshape(nx, nk, rows, step)
        for d in range(1, nx if x_first else nk):
            if x_first:
                out1[d - 1] = full[at_x(d)].astype(kind)
            else:
                for xx in range(nx):
                    out1[d - 1, xx] = full[xx, at_k(d)].astype(kind)

    def first_hop(i):
        x_first = parts[i][2]
        full, out1, in1, out2, in2, sems = bufs[i]
        return [
            send(out1.at[d - 1], in1.at[d - 1], sems.at[0, d], sems.at[1, d], plane[(d, 0) if x_first else (0, d)])
            for d in range(1, nx if x_first else nk)
        ]

    def second_hop(i, copies):
        start, cols, x_first, kind = parts[i]
        full, out1, in1, out2, in2, sems = bufs[i]
        n1, n2 = (nx, nk) if x_first else (nk, nx)
        for copy in copies:
            copy.wait_recv()

        def summed(other):
            total = full[x, other] if x_first else full[other, k]
            for d in range(n1 - 1):
                total = total + in1[d, other].astype(F32)
            return total

        second = []
        for d in range(1, n2):
            out2[d - 1] = summed(at_k(d) if x_first else at_x(d)).astype(kind)
            peer = plane[(0, d) if x_first else (d, 0)]
            second.append(send(out2.at[d - 1], in2.at[d - 1], sems.at[2, d], sems.at[3, d], peer))
        return summed(k if x_first else x), second

    def last(i, total, second):
        in2 = bufs[i][4]
        for d, copy in enumerate(second):
            copy.wait_recv()
            total = total + in2[d].astype(F32)
        return total.astype(BF16)

    half = width // 2
    multiply(0)
    hop_a = first_hop(0)
    multiply(1)
    hop_b = first_hop(1)
    multiply(2)
    multiply(3)
    sum_a = second_hop(0, hop_a)
    sum_b = second_hop(1, hop_b)
    hop_k = first_hop(2)
    hop_v = first_hop(3)
    qall[k, :, :half] = last(0, *sum_a)
    qall[k, :, half:] = last(1, *sum_b)
    q_copies = [
        send(qall.at[k], qall.at[k], qs.at[d], qr.at[d], plane[(0, d)]) for d in range(1, nk)
    ]
    for load in loads:
        load.wait()

    contract = (((1,), (1,)), ((), ()))
    place = k * keys + lax.broadcasted_iota(jnp.int32, (1, keys), 1)
    bias = jnp.where((place >= start_ref[0]) & (place < end_ref[0]), 0.0, LOW)
    lane = lax.broadcasted_iota(jnp.int32, (rows, HD), 1)

    def resident(block, begin, end):
        together = 2 if (end - begin) % 2 == 0 else 1

        @pl.loop(0, (end - begin) // together)
        def _(step):
            first = begin + step * together
            columns = [
                pl.ds(pl.multiple_of((first + m) * HD, HD), HD) for m in range(together)
            ]
            scores = [
                lax.dot_general(
                    qall[block, :, cols], ck[:, cols], contract, preferred_element_type=F32
                ) + bias
                for cols in columns
            ]
            peaks = [jnp.maximum(jnp.max(each, axis=1, keepdims=True), FLOOR) for each in scores]
            stats = stat[block]
            for m, cols in enumerate(columns):
                weights = jnp.exp2((scores[m] - peaks[m]) * RATE).astype(BF16)
                total = jnp.sum(weights.astype(F32), axis=1, keepdims=True)
                mix[block, :, cols] = jnp.dot(weights, cv[:, cols], preferred_element_type=F32)
                n = first + m
                stats = jnp.where(lane == n, peaks[m], jnp.where(lane == n + HD // 2, total, stats))
            stat[block] = stats

    def fresh(block, target):
        query_place = block * rows + lax.broadcasted_iota(jnp.int32, (rows, rows), 0)
        new_place = k * rows + lax.broadcasted_iota(jnp.int32, (rows, rows), 1)
        usable = new_place <= query_place
        stats = stat[block]
        merged = stats
        spots = [pl.ds(n * HD, HD) for n in range(heads)]
        scores = [
            jnp.where(
                usable,
                lax.dot_general(qall[block, :, cols], pair[:, cols], contract, preferred_element_type=F32),
                LOW,
            )
            for cols in spots
        ]
        weights, shrinks = [], []
        for n in range(heads):
            before = stats[:, n:n + 1]
            peak = jnp.maximum(before, jnp.max(scores[n], axis=1, keepdims=True))
            weights.append(jnp.exp2((scores[n] - peak) * RATE).astype(BF16))
            shrinks.append(jnp.exp2((before - peak) * RATE))
            total = stats[:, n + HD // 2:n + HD // 2 + 1] * shrinks[n] + jnp.sum(
                weights[n].astype(F32), axis=1, keepdims=True
            )
            merged = jnp.where(lane == n, peak, jnp.where(lane == n + HD // 2, total, merged))
        products = [
            jnp.dot(weights[n], pair[:, pl.ds(width + n * HD, HD)], preferred_element_type=F32)
            for n in range(heads)
        ]
        for n, cols in enumerate(spots):
            value = mix[block, :, cols] * shrinks[n] + products[n]
            if target is None:
                mix[block, :, cols] = value
            else:
                target[:, cols] = value.astype(BF16)
        stat[block] = merged

    stat[...] = jnp.zeros_like(stat)
    resident(k, 0, heads)
    for copy in q_copies:
        copy.wait_recv()
    for d in range(1, nk - 1):
        resident(at_k(d), 0, heads)
    if nk > 1:
        resident(at_k(nk - 1), 0, heads // 2)
    sum_k = second_hop(2, hop_k)
    sum_v = second_hop(3, hop_v)
    if nk > 1:
        resident(at_k(nk - 1), heads // 2, heads)
    pair[:, :width] = last(2, *sum_k)
    pair[:, width:] = last(3, *sum_v)
    part_rows = rows // 2
    spans = [pl.ds(r * part_rows, part_rows) for r in range(2)]
    arrivals, mix_copies = [], []
    for d in range(1, nk):
        other = at_k(d)
        fresh(other, mixs.at[d - 1])
        arrivals.append(send(stat.at[other], statr.at[d - 1], ss_.at[d], sr_.at[d], plane[(0, d)]))
        for r, span in enumerate(spans):
            mix_copies.append(send(
                mixs.at[d - 1, span], mixr.at[d - 1, span], ms.at[d, r], mr.at[d, r], plane[(0, d)]
            ))
    fresh(k, None)
    for copy in arrivals:
        copy.wait_recv()

    def tops(stats):
        return stats[:, :heads]

    def sums(stats):
        return stats[:, HD // 2:HD // 2 + heads]

    own_stat = stat[k]
    highest = tops(own_stat)
    for d in range(nk - 1):
        highest = jnp.maximum(highest, tops(statr[d]))
    factors = [jnp.exp2((tops(own_stat) - highest) * RATE)]
    total = sums(own_stat) * factors[0]
    for d in range(nk - 1):
        factors.append(jnp.exp2((tops(statr[d]) - highest) * RATE))
        total = total + sums(statr[d]) * factors[-1]
    away = [o for o in offsets if o != (0, 0)]
    b_copies = []
    for r, span in enumerate(spans):
        for d in range(nk - 1):
            mix_copies[2 * d + r].wait_recv()
        low, high = r * part_rows, (r + 1) * part_rows
        for n in range(heads):
            cols = pl.ds(n * HD, HD)
            value = mix[k, span, cols] * factors[0][low:high, n:n + 1]
            for d in range(nk - 1):
                value = value + mixr[d, span, cols].astype(F32) * factors[d + 1][low:high, n:n + 1]
            att[span, cols] = (value / total[low:high, n:n + 1]).astype(BF16)
        b_copies.append([
            send(att.at[span], attg.at[i, span], bs.at[i, r], br.at[i, r], plane[o]) for i, o in enumerate(away)
        ])
    o_local.wait()
    o_copy.wait_recv()
    relays = []

    def relay(piece, i, o, core, r):
        index = (2 * at_x(o[0]) + core) * nk + at_k(o[1])
        target, j = index // per_slot, lax.rem(index, per_slot)
        here = target == h
        far = pltpu.make_async_remote_copy(
            src_ref=piece, dst_ref=got.at[h, j, r], send_sem=vs.at[i, core, r], recv_sem=vr.at[h, j, r],
            device_id={"head": target}, device_id_type=MESH,
        )
        near = pltpu.make_async_copy(piece, got.at[h, j, r], vr.at[h, j, r])

        @pl.when(here)
        def _():
            near.start()

        @pl.when(jnp.logical_not(here))
        def _():
            far.start()

        relays.append((here, far))

    for r, span in enumerate(spans):
        for core in range(2):
            town[core, span] = jnp.dot(att[span], wo[core], preferred_element_type=F32).astype(BF16)
            relay(town.at[core, span], len(away), (0, 0), core, r)
    t_copies = {}
    for r, span in enumerate(spans):
        for i, o in enumerate(away):
            b_copies[r][i].wait_recv()
            back = plane[((nx - o[0]) % nx, (nk - o[1]) % nk)]
            for core in range(2):
                tsend[i, core, span] = jnp.dot(attg[i, span], wo[core], preferred_element_type=F32).astype(BF16)
                t_copies[r, i, core] = send(
                    tsend.at[i, core, span], tin.at[i, core, span], ts.at[i, core, r], tr.at[i, core, r], back
                )
    for r, span in enumerate(spans):
        for i, o in enumerate(away):
            for core in range(2):
                t_copies[r, i, core].wait_recv()
                relay(tin.at[i, core, span], i, o, core, r)
    for r, span in enumerate(spans):
        for j in range(per_slot):
            total = None
            for d in range(nh):
                origin = lax.rem(h + d, nh)
                pltpu.make_async_copy(got.at[origin, j, r], got.at[origin, j, r], vr.at[origin, j, r]).wait()
                part = got[origin, j, r].astype(F32)
                total = part if total is None else total + part
            out[span, j * depth:(j + 1) * depth] = total.astype(BF16)

    for copy in pending:
        copy.wait_send()
    for gone, copy in forwards + line:
        @pl.when(gone)
        def _():
            copy.wait_send()

    for here, far in relays:
        @pl.when(jnp.logical_not(here))
        def _():
            far.wait_send()


def attend_block(ns, nh, nk, tokens, wq, wkv, w_out, cache_keys, cache_values, key_start, key_end):
    rows, width = tokens.shape
    depth = wq.shape[0]
    keys = cache_keys.shape[1]
    nx = ns // 2
    group = nx * nk
    more = max(nk - 1, 1)
    dma = pltpu.SemaphoreType.DMA
    far = group - 1
    scratch = [
        pltpu.VMEM((2, width, depth), BF16),
        pltpu.VMEM((rows, width), BF16),
        pltpu.VMEM((far, rows, width), BF16),
        pltpu.VMEM((2, rows, depth), BF16),
        pltpu.VMEM((far, 2, rows, depth), BF16),
        pltpu.VMEM((far, 2, rows, depth), BF16),
        pltpu.VMEM((nh, width // depth, 2, rows // 2, depth), BF16),
        dma, dma, dma,
        dma((far, 2)), dma((far, 2)),
        dma((far, 2, 2)), dma((far, 2, 2)),
        dma((group, 2, 2)), dma((nh, width // depth, 2)),
        pltpu.VMEM((nh - 1, rows, width), BF16),
        pltpu.VMEM((nh - 1, rows, width), BF16),
        pltpu.VMEM(wkv.shape, BF16),
        pltpu.VMEM((8, rows), F32),
        pltpu.VMEM((nh - 1, 8, rows), F32),
        pltpu.VMEM((2, depth, 3 * width), BF16),
        pltpu.VMEM((group, 2, rows, depth), BF16),
        pltpu.VMEM((2, group * rows, depth), BF16),
        pltpu.VMEM((8, rows), F32),
        pltpu.VMEM((group, 8, rows), F32),
        pltpu.VMEM((nk, rows, width), BF16),
        pltpu.VMEM((keys, width), BF16),
        pltpu.VMEM((keys, width), BF16),
        pltpu.VMEM((rows, 2 * width), BF16),
        pltpu.VMEM((nk, rows, width), F32),
        pltpu.VMEM((nk, rows, HD), F32),
        pltpu.VMEM((more, rows, width), BF16),
        pltpu.VMEM((more, rows, width), BF16),
        pltpu.VMEM((more, rows, HD), F32),
        dma((2, nh - 1, width // depth)), dma((2, nh - 1, width // depth)), dma,
        dma((nh - 1,)), dma((nh - 1,)),
        dma((2,)), dma((2,)), dma,
        dma((group,)), dma((group,)),
        dma((2 * nh - 1, width // depth)), dma((group, 2)),
        dma((nk,)), dma((nk,)),
        dma((2,)),
        dma((nk, 2)), dma((nk, 2)), dma((nk,)), dma((nk,)),
    ]
    for start, cols, x_first, kind in split_parts(width):
        n1, n2 = (nx, nk) if x_first else (nk, nx)
        scratch += [
            pltpu.VMEM((nx, nk, rows, cols), F32),
            pltpu.VMEM((max(n1 - 1, 1), n2, rows, cols), kind),
            pltpu.VMEM((max(n1 - 1, 1), n2, rows, cols), kind),
            pltpu.VMEM((max(n2 - 1, 1), rows, cols), kind),
            pltpu.VMEM((max(n2 - 1, 1), rows, cols), kind),
            dma((4, max(n1, n2))),
        ]
    vmem = pl.BlockSpec(memory_space=pltpu.VMEM)
    smem = pl.BlockSpec(memory_space=pltpu.SMEM)
    hbm = pl.BlockSpec(memory_space=pl.ANY)
    return pl.pallas_call(
        functools.partial(block_kernel, ns, nh, nk),
        out_shape=jax.ShapeDtypeStruct((rows, width), BF16),
        in_specs=[vmem, hbm, hbm, hbm, hbm, hbm, smem, smem],
        out_specs=vmem,
        scratch_shapes=scratch,
        compiler_params=pltpu.CompilerParams(
            collective_id=0, has_side_effects=True, vmem_limit_bytes=60 * 1024 * 1024
        ),
        name="attend_block",
    )(tokens, wq, wkv, w_out, cache_keys, cache_values, key_start, key_end)


def shards(ns, nh, nk, tokens, w_query, w_keyvalue, cache_keys, cache_values, key_start, key_end, w_out):
    return attend_block(
        ns, nh, nk, tokens[0], w_query, w_keyvalue, w_out, cache_keys, cache_values, key_start, key_end
    )[None]


def solution(mesh):
    placed = (
        P("section", "kv", "head"),
        P(("section", "kv"), "head"),
        P(("section", "kv"), None, "head"),
        P("section", "kv", "head"),
        P("section", "kv", "head"),
        P("section"),
        P("section"),
        P("head", ("section", "kv")),
    )
    body = functools.partial(shards, mesh.shape["section"], mesh.shape["head"], mesh.shape["kv"])
    return jax.shard_map(
        body, mesh=mesh, in_specs=placed, out_specs=P("section", "kv", "head"), check_vma=False
    )
```
